256 devices in a mesh: head: 8 (over y, x_lo), tok: 32 (over x_hi, z, core).
Axes of the slice: x: 4 (x_hi: 2, x_lo: 2; x = x_hi * 2 + x_lo), y: 4, z: 8, core: 2. Of those that a mesh axis runs over, the one named last changes fastest.
Arguments:
- head_outputs: bfloat16 [1024, 8192], P('tok', 'head'), may hold values from -6 to 6
- dec_bias: float32 [8192], P('head'), may hold values from -3 to 3
- enc_bias: float32 [65536], P('tok'), may hold values from -3 to 3
- enc_weight: bfloat16 [8192, 65536], P('head', 'tok'), may hold values from -0.0625 to 0.0625
- dec_weight: bfloat16 [65536, 8192], P('tok', 'head'), may hold values from -0.75 to 0.75
- out_weight: bfloat16 [8192, 8192], P('head', 'tok'), may hold values from -0.0625 to 0.0625
- active_ids: int32 [1024, 128], replicated, may hold values from 0 to 65535, as said below
Outputs:
- reconstruction: bfloat16 [1024, 8192], P('tok', 'head')
- projected: bfloat16 [1024, 8192], P('tok', 'head')
The draws below stay inside these ranges and needn't reach their ends.
Inputs may be any that keep to these rules, and one draw needn't show every extreme that they name: `active_ids`: entry j of each row lies among the latents j * 512 to (j + 1) * 512 - 1, so the 128 entries of a row are different.
All inputs are finite; a program needn't handle non-finite values.
Results may differ from the reference program's by a relative error of at most 0.0061.
Values may be sent and summed in bfloat16 or wider, within the bound.
A program may use at most 128 MiB of HBM per device.

```python
import jax
import jax.numpy as jnp

Z = 8192
D = 8192
LAT = 65536
K = 128
TOKENS = 1024


def draw_active_ids(key, part):
    stride = LAT // K
    offsets = jax.random.randint(jax.random.fold_in(key, 11), (TOKENS, K), 0, stride, dtype=jnp.int32)
    bases = (jnp.arange(K, dtype=jnp.int32) * stride)[None, :]
    row_pos = jnp.arange(TOKENS, dtype=jnp.int32)[:, None]
    col_pos = jnp.arange(K, dtype=jnp.int32)[None, :]
    first = (row_pos == 0) & (col_pos == 0)
    final = (row_pos == TOKENS - 1) & (col_pos == K - 1)
    offsets = jnp.where(first, 0, offsets)
    offsets = jnp.where(final, stride - 1, offsets)
    return (bases + offsets).astype(jnp.int32)


def block_scale(own_key, dims, pieces, least, largest):
    factor_of = 1.0
    for position, blocks in pieces:
        steps = jax.random.uniform(jax.random.fold_in(jax.random.fold_in(own_key, 6), position), (blocks,), jnp.float32, least / len(pieces), largest / len(pieces))
        factor_of = factor_of * jnp.repeat(jnp.exp(steps), dims[position] // blocks).reshape((-1,) + (1,) * (len(dims) - 1 - position))
    return factor_of


def scatter_about(key, dims, scale, most, cuts=(), kind=jnp.bfloat16):
    result = scale * jax.random.normal(key, dims, jnp.float32)
    if cuts:
        result = result * block_scale(key, dims, cuts, -0.22, 0.18)
    return jnp.clip(result, -most, most).astype(kind)


def setup_inputs(seed: int = 0) -> dict:
    key_of = jax.random.split(jax.random.key(seed), 8)
    return {
        "head_outputs": scatter_about(key_of[0], (TOKENS, Z), 1.0, 6.0, ((0, 32), (1, 8))),
        "dec_bias": scatter_about(key_of[1], (Z,), 0.5, 3.0, ((0, 8),), jnp.float32),
        "enc_bias": scatter_about(key_of[2], (LAT,), 0.5, 3.0, ((0, 32),), jnp.float32),
        "enc_weight": scatter_about(key_of[3], (Z, LAT), Z ** -0.5, 0.0625, ((0, 8), (1, 32))),
        "dec_weight": scatter_about(key_of[4], (LAT, Z), (K // 2) ** -0.5, 0.75, ((0, 32), (1, 8))),
        "out_weight": scatter_about(key_of[5], (Z, D), Z ** -0.5, 0.0625, ((0, 8), (1, 32))),
        "active_ids": draw_active_ids(jax.random.fold_in(key_of[7], 71), 0),
    }


def reference(head_outputs, dec_bias, enc_bias, enc_weight, dec_weight, out_weight, active_ids):
    centered = (head_outputs.astype(jnp.float32) - dec_bias[None, :]).astype(jnp.bfloat16)
    pre = jnp.dot(centered, enc_weight, preferred_element_type=jnp.float32) + enc_bias[None, :]
    row_ids = jnp.arange(active_ids.shape[0], dtype=jnp.int32)[:, None]
    mask = jnp.zeros(pre.shape, jnp.float32).at[row_ids, active_ids].set(1.0)
    latents = (mask * jnp.maximum(pre, 0.0)).astype(jnp.bfloat16)
    recon = jnp.dot(latents, dec_weight, preferred_element_type=jnp.float32) + dec_bias[None, :]
    reconstruction = recon.astype(jnp.bfloat16)
    projected = jnp.dot(reconstruction, out_weight, preferred_element_type=jnp.float32).astype(jnp.bfloat16)
    return (reconstruction, projected)
```

```python
import jax
import jax.numpy as jnp
from jax import lax
from jax.sharding import PartitionSpec as P


def on_device(head_outputs, dec_bias, enc_bias, enc_weight, dec_weight, out_weight, active_ids):
    tokens, per_token = active_ids.shape
    lat_count = enc_weight.shape[1]
    stride = lat_count * lax.axis_size("tok") // per_token
    here = lat_count // stride
    tok = lax.axis_index("tok")

    centered = (head_outputs.astype(jnp.float32) - dec_bias[None, :]).astype(jnp.bfloat16)
    partial_pre = jnp.dot(
        lax.all_gather(centered, "tok", axis=0, tiled=True),
        enc_weight,
        preferred_element_type=jnp.float32,
    ).reshape(tokens, here, stride)
    ids = lax.dynamic_slice(active_ids, (0, tok * here), (tokens, here))
    offset = ids - (tok * here + jnp.arange(here, dtype=jnp.int32))[None, :] * stride
    active = offset[:, :, None] == jnp.arange(stride, dtype=jnp.int32)[None, None, :]
    picked = jnp.sum(jnp.where(active, partial_pre, 0.0), axis=2)
    bias = jnp.sum(jnp.where(active, enc_bias.reshape(1, here, stride), 0.0), axis=2)
    value = jnp.maximum(lax.psum(picked, "head") + bias, 0.0)
    latents = jnp.where(active, value[:, :, None], 0.0).astype(jnp.bfloat16)
    decoded = lax.psum_scatter(
        jnp.dot(latents.reshape(tokens, lat_count), dec_weight, preferred_element_type=jnp.float32),
        "tok",
        scatter_dimension=0,
        tiled=True,
    )
    reconstruction = (decoded + dec_bias[None, :]).astype(jnp.bfloat16)
    partial_out = jnp.dot(
        lax.all_gather(reconstruction, "tok", axis=0, tiled=True),
        out_weight,
        preferred_element_type=jnp.float32,
    )
    mine = lax.all_to_all(partial_out, "tok", split_axis=0, concat_axis=1, tiled=True)
    projected = lax.psum_scatter(mine, "head", scatter_dimension=1, tiled=True).astype(jnp.bfloat16)
    return (reconstruction, projected)


def solution(mesh):
    return jax.shard_map(
        on_device,
        mesh=mesh,
        in_specs=(
            P("tok", "head"),
            P("head"),
            P("tok"),
            P("head", "tok"),
            P("tok", "head"),
            P("head", "tok"),
            P(),
        ),
        out_specs=(P("tok", "head"), P("tok", "head")),
        check_vma=False,
    )
```

```python
import jax
import jax.numpy as jnp
from jax import lax
from jax.experimental import pallas as pl
from jax.experimental.pallas import tpu as pltpu
from jax.sharding import PartitionSpec as P

MESH = pl.DeviceIdType.MESH
F32, BF16 = jnp.float32, jnp.bfloat16

HEADS = 8
TOKENS, WIDTH, BLOCK = 1024, 1024, 32
LATS, HERE, STRIDE = 2048, 4, 512
COLS = 256
PLANE = 128
PLANES = (0, -1, 1, -2, 2, -3, 3, 4)
GROUPS = ((0, 1), (1, 2), (3, 2), (5, 2), (7, 1))
MESSAGES = 192


def row_of(slot, core, side):
    return PLANE * slot + 64 * core + BLOCK * side


def kernel(
    ho, dbias, ebias, ew, dw, ow, ids,
    rec_out, proj_out,
    ho_v, db_v, eb_v, ew_v, dw_v, ow_v, ids_v,
    cen, off, vals, packed, lat, own_part, core_out, core_in,
    zp_out, zp_in, zm_out, zm_in, x_out, x_in, rec,
    part, part_in, piece, piece_in, proj_v,
    load_sem, send_sem, recv_sem, last_recv, store_sem,
):
    h = lax.axis_index("head")
    t = lax.axis_index("tok")
    core, z, side = t % 2, (t // 2) % 8, t // 16

    def tok_of(dside, dz, dcore):
        return ((side + dside) % 2) * 16 + ((z + dz) % 8) * 2 + (core + dcore) % 2

    zp, zm = {"tok": tok_of(0, 1, 0)}, {"tok": tok_of(0, 7, 0)}
    xn, cn = {"tok": tok_of(1, 0, 0)}, {"tok": tok_of(0, 0, 1)}
    heads = [(h + k) % HEADS for k in range(HEADS)]
    out_head = t // 4
    my_part = h // 2
    final_tok = [tok_of(my_part % 2, PLANES[s] % 8, my_part // 2) for s in range(8)]
    to_self = (out_head == h) & (my_part == 0)

    loads = []
    for n, (src, dst) in enumerate(
        ((ho, ho_v), (dbias, db_v), (ids, ids_v), (ebias, eb_v), (ew, ew_v), (dw, dw_v), (ow, ow_v))
    ):
        loads.append(pltpu.make_async_copy(src, dst, load_sem.at[n]))
        loads[-1].start()

    barrier = pltpu.get_barrier_semaphore()
    for target in (zp, zm, xn, cn):
        pl.semaphore_signal(barrier, inc=1, device_id=target, device_id_type=MESH)
    for k in range(1, HEADS):
        pl.semaphore_signal(barrier, inc=1, device_id={"head": heads[k]}, device_id_type=MESH)
    for s in range(8):
        target = {"head": out_head, "tok": final_tok[s]}
        pl.semaphore_signal(barrier, inc=1, device_id=target, device_id_type=MESH)

    loads[0].wait()
    loads[1].wait()
    cen[pl.ds(0, BLOCK), :] = (ho_v[...].astype(F32) - db_v[...]).astype(BF16)
    vals[...] = jnp.zeros_like(vals)
    pl.semaphore_wait(barrier, 4 + 7 + 8)

    sent = []

    def send(src, dst, target):
        n = len(sent)
        copy = pltpu.make_async_remote_copy(
            src_ref=src, dst_ref=dst, send_sem=send_sem.at[n], recv_sem=recv_sem.at[n],
            device_id=target, device_id_type=MESH,
        )
        copy.start()
        sent.append(copy)
        return copy

    def gather(buf, crossed):
        def block(slot, core, side):
            return buf.at[pl.ds(row_of(slot, core, side), BLOCK), :]

        def cross(slot, side):
            crossed[slot, side] = send(block(slot, 0, side), block(slot, 1, side), cn)

        plus, minus = {}, {}

        def go_plus(k, side):
            if k == 3 and side == 1:
                return
            plus[k, side] = send(
                block(2 * k - 1 if k else 0, 0, side), block(2 * k + 1, 0, side), zp
            )

        def go_minus(k, side):
            if k == 3 and side == 0:
                return
            minus[k, side] = send(
                block(2 * k, 0, side), block(2 * k + 2 if k < 3 else 7, 0, side), zm
            )

        over = send(block(0, 0, 0), block(0, 0, 1), xn)
        go_plus(0, 0)
        go_minus(0, 0)
        cross(0, 0)
        yield
        over.wait_recv()
        go_plus(0, 1)
        go_minus(0, 1)
        cross(0, 1)
        yield
        for k in range(1, 4):
            for side in range(2):
                plus[k - 1, side].wait_recv()
                go_plus(k, side)
                cross(2 * k - 1, side)
                minus[k - 1, side].wait_recv()
                go_minus(k, side)
                cross(2 * k, side)
                yield
        plus[3, 0].wait_recv()
        cross(7, 0)
        minus[3, 1].wait_recv()
        cross(7, 1)
        yield

    def whole(crossed, slots):
        for slot in slots:
            for side in range(2):
                crossed[slot, side].wait_recv()

    lane = lax.broadcasted_iota(jnp.int32, (PLANE, 128), 1)
    lane_f = lane.astype(F32)

    crossed = {}
    steps = gather(cen, crossed)
    next(steps)
    loads[2].wait()

    def offsets(slot):
        row = lambda q: pl.multiple_of(
            ((side + q % 2) % 2) * 512 + ((z + PLANES[slot] % 8) % 8) * 64 + ((core + q // 2) % 2) * BLOCK,
            BLOCK,
        )
        here = jnp.concatenate([ids_v[pl.ds(row(q), BLOCK), :] for q in range(4)], axis=0)
        here = (here - t * LATS).astype(F32)
        for j in range(HERE):
            column = jnp.sum(jnp.where(lane == t * HERE + j, here, 0.0), axis=1, keepdims=True)
            off[j, pl.ds(PLANE * slot, PLANE), :] = jnp.broadcast_to(column - j * STRIDE, (PLANE, 128))

    for slot in range(4):
        offsets(slot)
    next(steps)
    for slot in range(4, 8):
        offsets(slot)
    loads[3].wait()
    eb_v[...] = eb_v[...] * jnp.where(h == 0, 1.0, 0.0)

    def encode(group, first, last):
        slot, count = group
        rows = pl.ds(PLANE * slot, PLANE * count)
        lane_g = lax.broadcasted_iota(jnp.int32, (PLANE * count, 128), 1)
        lane_gf = lane_g.astype(F32)

        def body(j, carry):
            lats = pl.ds(pl.multiple_of(j * STRIDE, STRIDE), STRIDE)
            pre = jnp.dot(cen[rows, :], ew_v[:, lats], preferred_element_type=F32) + eb_v[:, lats]
            where = off[j, rows, :]
            total = jnp.zeros((PLANE * count, 128), F32)
            for q in range(4):
                total += jnp.where(lane_gf + 128.0 * q == where, pre[:, 128 * q:128 * (q + 1)], 0.0)
            picked = jnp.sum(total, axis=1, keepdims=True)
            vals[rows, :] += jnp.where(lane_g == j, picked, 0.0)
            return carry

        lax.fori_loop(first, last, body, 0)

    def pack(slot):
        packed[0, :, pl.ds(PLANE * slot, PLANE)] = vals[pl.ds(PLANE * slot, PLANE), :].T[:8, :]

    def pack(slots):
        for slot in slots:
            rows = pl.ds(PLANE * slot, PLANE)
            packed[0, :, rows] = vals[rows, :].T[:8, :]
        lanes = pl.ds(PLANE * slots[0], PLANE * len(slots))
        for k in range(1, HEADS):
            arrived[slots[0], k] = send(
                packed.at[0, :, lanes], packed.at[k, :, lanes], {"head": heads[k]}
            )

    arrived = {}
    loads[4].wait()
    for n in range(3):
        slot, count = GROUPS[n]
        next(steps)
        whole(crossed, range(slot, slot + count))
        encode(GROUPS[n], 0, 2)
        next(steps)
        encode(GROUPS[n], 2, 4)
    next(steps)
    pack(range(0, 5))
    whole(crossed, (5, 6))
    encode(GROUPS[3], 0, 4)
    pack((5, 6))
    whole(crossed, (7,))
    encode(GROUPS[4], 0, 4)
    pack((7,))

    loads[5].wait()
    crossed_sums = {}

    def decode(group):
        slot, count = group

        def fill(i, carry):
            rows = pl.ds(pl.multiple_of(PLANE * (slot + i), PLANE), PLANE)
            total = packed[0, :, rows]
            for k in range(1, HEADS):
                total += packed[k, :, rows]
            value = jnp.concatenate(
                [jnp.maximum(total, 0.0), jnp.zeros((PLANE - 8, PLANE), F32)], axis=0
            ).T
            for j in range(HERE):
                column = jnp.broadcast_to(value[:, j:j + 1], (PLANE, 128))
                where = off[j, rows, :]
                for q in range(4):
                    lat[pl.ds(pl.multiple_of(PLANE * i, PLANE), PLANE),
                        STRIDE * j + 128 * q:STRIDE * j + 128 * (q + 1)] = jnp.where(
                            lane_f + 128.0 * q == where, column, 0.0).astype(BF16)
            return carry

        lax.fori_loop(0, count, fill, 0)

        def body(n, carry):
            cols = pl.ds(pl.multiple_of(n * 256, 256), 256)
            total = jnp.dot(lat[pl.ds(0, PLANE * count), :], dw_v[:, cols], preferred_element_type=F32)
            for i in range(count):
                own_part[slot + i, :, cols] = total[PLANE * i:PLANE * i + 64]
                core_out[slot + i, :, cols] = total[PLANE * i + 64:PLANE * (i + 1)].astype(BF16)
            return carry

        lax.fori_loop(0, WIDTH // 256, body, 0)
        for i in range(count):
            crossed_sums[slot + i] = send(core_out.at[slot + i], core_in.at[slot + i], cn)

    def summed(slot, side):
        rows = pl.ds(BLOCK * side, BLOCK)
        return own_part[slot, rows, :] + core_in[slot, rows, :].astype(F32)

    plus, minus = {}, {}

    def ring(out, arrived_at, table, target, n, slot, side, before):
        total = summed(slot, side)
        if before is not None:
            table[before].wait_recv()
            total += arrived_at[before].astype(F32)
        out[n] = total.astype(BF16)
        table[n] = send(out.at[n], arrived_at.at[n], target)

    def go_plus(n, slot, side, before):
        ring(zp_out, zp_in, plus, zp, n, slot, side, before)

    def go_minus(n, slot, side, before):
        ring(zm_out, zm_in, minus, zm, n, slot, side, before)

    def get(slot):
        for k in range(1, HEADS):
            arrived[slot, k].wait_recv()

    get(7)
    decode((7, 1))
    get(5)
    crossed_sums[7].wait_recv()
    go_plus(0, 7, 1, None)
    go_minus(0, 7, 0, None)
    decode((5, 2))
    get(0)
    crossed_sums[5].wait_recv()
    crossed_sums[6].wait_recv()
    go_plus(2, 6, 0, None)
    go_minus(1, 5, 1, None)
    go_plus(1, 6, 1, 0)
    go_minus(2, 5, 0, 0)
    decode((3, 2))
    crossed_sums[3].wait_recv()
    crossed_sums[4].wait_recv()
    go_minus(3, 3, 1, 1)
    go_plus(4, 4, 0, 2)
    go_plus(3, 4, 1, 1)
    go_minus(4, 3, 0, 2)
    decode((1, 2))
    crossed_sums[1].wait_recv()
    crossed_sums[2].wait_recv()
    go_minus(5, 1, 1, 3)
    go_plus(5, 2, 1, 3)
    go_plus(6, 2, 0, 4)
    go_minus(6, 1, 0, 4)
    decode((0, 1))
    crossed_sums[0].wait_recv()

    def own(side, n):
        plus[n].wait_recv()
        minus[n].wait_recv()
        return summed(0, side) + (zp_in[n].astype(F32) + zm_in[n].astype(F32))

    x_out[...] = own(1, 5).astype(BF16)
    x_sum = send(x_out, x_in, xn)
    mine = own(0, 6) + db_v[...]
    x_sum.wait_recv()
    rec[pl.ds(0, BLOCK), :] = (mine + x_in[...].astype(F32)).astype(BF16)

    crossed = {}
    steps = gather(rec, crossed)
    next(steps)
    store_rec = pltpu.make_async_copy(rec.at[pl.ds(0, BLOCK), :], rec_out, store_sem.at[0])
    store_rec.start()
    loads[6].wait()
    spread = {}

    def project(group):
        slot, count = group
        out = jnp.dot(
            rec[pl.ds(PLANE * slot, PLANE * count), :], ow_v[...], preferred_element_type=F32
        ).astype(BF16)
        for i in range(count):
            part[slot + i] = out[PLANE * i:PLANE * (i + 1)]
        for k in range(1, HEADS):
            rows = pl.ds(pl.multiple_of(heads[k] * 16, 16), 16)
            spread[slot, k] = send(
                part.at[pl.ds(slot, count), rows, :],
                part_in.at[k, pl.ds(slot, count)],
                {"head": heads[k]},
            )

    def finish(group):
        slot, count = group
        for k in range(1, HEADS):
            spread[slot, k].wait_recv()
        rows = pl.ds(pl.multiple_of(h * 16, 16), 16)
        for s in range(slot, slot + count):
            total = part[s, rows, :].astype(F32)
            for k in range(1, HEADS):
                total += part_in[k, s].astype(F32)
            piece[s] = total.astype(BF16)
            n = len(sent)
            sent.append(None)
            copy = pltpu.make_async_remote_copy(
                src_ref=piece.at[s],
                dst_ref=piece_in.at[t % 4, h % 2],
                send_sem=send_sem.at[n],
                recv_sem=last_recv.at[t % 4, h % 2],
                device_id={"head": out_head, "tok": final_tok[s]},
                device_id_type=MESH,
            )
            if s:
                copy.start()
                sent[n] = copy
                continue
            local = pltpu.make_async_copy(piece.at[0], piece_in.at[t % 4, h % 2], last_recv.at[t % 4, h % 2])

            @pl.when(to_self)
            def _():
                local.start()

            @pl.when(jnp.logical_not(to_self))
            def _():
                copy.start()

            own_piece.append(copy)

    own_piece = []
    next(steps)
    for n in range(3):
        slot, count = GROUPS[n]
        next(steps)
        next(steps)
        whole(crossed, range(slot, slot + count))
        project(GROUPS[n])
        if n:
            finish(GROUPS[n - 1])
    next(steps)
    whole(crossed, (5, 6))
    project(GROUPS[3])
    finish(GROUPS[2])
    whole(crossed, (7,))
    project(GROUPS[4])
    finish(GROUPS[3])
    finish(GROUPS[4])
    for copy in sent:
        if copy is not None:
            copy.wait_send()

    @pl.when(jnp.logical_not(to_self))
    def _():
        own_piece[0].wait_send()

    store_rec.wait()
    for j in range(4):
        for half in range(2):
            pltpu.make_async_copy(piece_in.at[j, half], piece_in.at[j, half], last_recv.at[j, half]).wait()
            proj_v[16 * half:16 * half + 16, COLS * j:COLS * (j + 1)] = piece_in[j, half]
    store_proj = pltpu.make_async_copy(proj_v, proj_out, store_sem.at[1])
    store_proj.start()
    store_proj.wait()


def on_device(head_outputs, dec_bias, enc_bias, enc_weight, dec_weight, out_weight, active_ids):
    block = jax.ShapeDtypeStruct((BLOCK, WIDTH), BF16)
    vmem = pltpu.VMEM
    return pl.pallas_call(
        kernel,
        out_shape=(block, block),
        in_specs=[pl.BlockSpec(memory_space=pl.ANY)] * 7,
        out_specs=(pl.BlockSpec(memory_space=pl.ANY),) * 2,
        scratch_shapes=[
            vmem((BLOCK, WIDTH), BF16),
            vmem((1, WIDTH), F32),
            vmem((1, LATS), F32),
            vmem((WIDTH, LATS), BF16),
            vmem((LATS, WIDTH), BF16),
            vmem((WIDTH, COLS), BF16),
            vmem((TOKENS, 128), jnp.int32),
            vmem((TOKENS, WIDTH), BF16),
            vmem((HERE, TOKENS, 128), F32),
            vmem((TOKENS, 128), F32),
            vmem((HEADS, 8, TOKENS), F32),
            vmem((2 * PLANE, LATS), BF16),
            vmem((8, 64, WIDTH), F32),
            vmem((8, 64, WIDTH), BF16),
            vmem((8, 64, WIDTH), BF16),
            vmem((7, BLOCK, WIDTH), BF16),
            vmem((7, BLOCK, WIDTH), BF16),
            vmem((7, BLOCK, WIDTH), BF16),
            vmem((7, BLOCK, WIDTH), BF16),
            vmem((BLOCK, WIDTH), BF16),
            vmem((BLOCK, WIDTH), BF16),
            vmem((TOKENS, WIDTH), BF16),
            vmem((8, PLANE, COLS), BF16),
            vmem((HEADS, 8, 16, COLS), BF16),
            vmem((8, 16, COLS), BF16),
            vmem((4, 2, 16, COLS), BF16),
            vmem((BLOCK, WIDTH), BF16),
            pltpu.SemaphoreType.DMA((7,)),
            pltpu.SemaphoreType.DMA((MESSAGES,)),
            pltpu.SemaphoreType.DMA((MESSAGES,)),
            pltpu.SemaphoreType.DMA((4, 2)),
            pltpu.SemaphoreType.DMA((2,)),
        ],
        compiler_params=pltpu.CompilerParams(
            collective_id=0, has_side_effects=True, vmem_limit_bytes=60 * 2 ** 20
        ),
        cost_estimate=pl.CostEstimate(flops=9 * 10 ** 9, bytes_accessed=9 * 2 ** 20, transcendentals=0),
    )(
        head_outputs,
        dec_bias.reshape(1, WIDTH),
        enc_bias.reshape(1, LATS),
        enc_weight,
        dec_weight,
        out_weight,
        active_ids,
    )


def solution(mesh):
    return jax.shard_map(
        on_device,
        mesh=mesh,
        in_specs=(
            P("tok", "head"),
            P("head"),
            P("tok"),
            P("head", "tok"),
            P("tok", "head"),
            P("head", "tok"),
            P(),
        ),
        out_specs=(P("tok", "head"), P("tok", "head")),
        check_vma=False,
    )
```

```python
import jax
import jax.numpy as jnp
from jax import lax
from jax.experimental import pallas as pl
from jax.experimental.pallas import tpu as pltpu
from jax.sharding import PartitionSpec as P

MESH = pl.DeviceIdType.MESH
F32, BF16 = jnp.float32, jnp.bfloat16

HEADS = 8
TOKENS, WIDTH, BLOCK = 1024, 1024, 32
LATS, HERE, STRIDE = 2048, 4, 512
COLS = 256
PLANE = 128
PLANES = (0, -1, 1, -2, 2, -3, 3, 4)
SLOT = {0: 0, -1: 1, 1: 2, -2: 3, 2: 4, -3: 5, 3: 6, -4: 7, 4: 7}
GROUPS = ((0, 1), (1, 2), (3, 2), (5, 2), (7, 1))
MESSAGES = 224


def row_of(slot, core, side):
    return PLANE * slot + 64 * core + BLOCK * side


def kernel(
    ho, dbias, ebias, ew, dw, ow, ids,
    rec_out, proj_out,
    ho_v, db_v, eb_v, ew_v, dw_v, ow_v, ids_v,
    cen, off, vals, packed, lat, own_part, core_out, core_in,
    zp_out, zp_in, zm_out, zm_in, x_out, x_in, rec, biases,
    part, part_in, piece, piece_in, proj_v,
    load_sem, send_sem, recv_sem, last_recv, store_sem,
):
    h = lax.axis_index("head")
    t = lax.axis_index("tok")
    core, z, side = t % 2, (t // 2) % 8, t // 16

    def tok_of(dside, dz, dcore):
        return ((side + dside) % 2) * 16 + ((z + dz) % 8) * 2 + (core + dcore) % 2

    zp, zm = {"tok": tok_of(0, 1, 0)}, {"tok": tok_of(0, 7, 0)}
    zp_other, zm_other = {"tok": tok_of(1, 1, 0)}, {"tok": tok_of(1, 7, 0)}
    xn, cn, far = {"tok": tok_of(1, 0, 0)}, {"tok": tok_of(0, 0, 1)}, {"tok": tok_of(0, 4, 0)}
    heads = [(h + k) % HEADS for k in range(HEADS)]
    out_head = t // 4
    my_part = h // 2
    final_tok = [tok_of(my_part % 2, PLANES[s] % 8, my_part // 2) for s in range(8)]
    to_self = (out_head == h) & (my_part == 0)

    loads = []
    for n, (src, dst) in enumerate(
        ((ho, ho_v), (dbias, db_v), (ids, ids_v), (ebias, eb_v), (ew, ew_v), (dw, dw_v), (ow, ow_v))
    ):
        loads.append(pltpu.make_async_copy(src, dst, load_sem.at[n]))
        loads[-1].start()

    barrier = pltpu.get_barrier_semaphore()
    for target in (zp, zm, zp_other, zm_other, xn, cn, far):
        pl.semaphore_signal(barrier, inc=1, device_id=target, device_id_type=MESH)
    for k in range(1, HEADS):
        pl.semaphore_signal(barrier, inc=1, device_id={"head": heads[k]}, device_id_type=MESH)
    for s in range(8):
        target = {"head": out_head, "tok": final_tok[s]}
        pl.semaphore_signal(barrier, inc=1, device_id=target, device_id_type=MESH)

    loads[0].wait()
    loads[1].wait()
    cen[pl.ds(0, BLOCK), :] = (ho_v[...].astype(F32) - db_v[...]).astype(BF16)

    lane = lax.broadcasted_iota(jnp.int32, (PLANE, 128), 1)
    lane_f = lane.astype(F32)

    def offsets(slot):
        def row(q):
            return pl.multiple_of(
                ((side + q % 2) % 2) * 512 + ((z + PLANES[slot] % 8) % 8) * 64 + ((core + q // 2) % 2) * BLOCK,
                BLOCK,
            )

        rows = pl.ds(PLANE * slot, PLANE)
        here = jnp.concatenate([ids_v[pl.ds(row(q), BLOCK), :] for q in range(4)], axis=0)
        here = (here - t * LATS).astype(F32)
        bias = jnp.zeros((PLANE, 128), F32)
        for j in range(HERE):
            column = jnp.sum(jnp.where(lane == t * HERE + j, here, 0.0), axis=1, keepdims=True) - j * STRIDE
            column = jnp.broadcast_to(column, (PLANE, 128))
            off[j, rows, :] = column
            total = jnp.zeros((PLANE, 128), F32)
            for q in range(4):
                first = STRIDE * j + 128 * q
                total += jnp.where(lane_f + 128.0 * q == column, eb_v[:, first:first + 128], 0.0)
            bias += jnp.where(lane == j, jnp.sum(total, axis=1, keepdims=True), 0.0)
        biases[rows, :] = bias

    loads[2].wait()
    loads[3].wait()
    for slot in range(8):
        offsets(slot)
    pl.semaphore_wait(barrier, 7 + 7 + 8)

    sent = []

    def send(src, dst, target):
        n = len(sent)
        copy = pltpu.make_async_remote_copy(
            src_ref=src, dst_ref=dst, send_sem=send_sem.at[n], recv_sem=recv_sem.at[n],
            device_id=target, device_id_type=MESH,
        )
        copy.start()
        sent.append(copy)
        return copy

    def gather(buf, crossed):
        def block(slot, core, side):
            return buf.at[pl.ds(row_of(slot, core, side), BLOCK), :]

        def cross(slot, side):
            crossed[slot, side] = send(block(slot, 0, side), block(slot, 1, side), cn)

        moved = {}

        def go(way, k, side, half):
            slot = SLOT[way * k]
            landing = SLOT[way * (k + 1)]
            if k == 0:
                src, side_there = part(0, 0, half), side
                target = ((zp, zp_other), (zm, zm_other))[way > 0][side]
            else:
                if k == 3 and side != (way > 0):
                    return
                src, side_there = part(slot, side, half), side
                target = (zp, zm)[way > 0]
            moved[way, k, side, half] = send(src, part(landing, side_there, half), target)

        def part(slot, side, half):
            return buf.at[pl.ds(row_of(slot, 0, side) + 16 * half, 16), :]

        for side in range(2):
            for half in range(2):
                for way in (-1, 1):
                    go(way, 0, side, half)
        over = send(block(0, 0, 0), block(0, 0, 1), xn)
        cross(0, 0)
        yield
        for k in range(1, 5):
            for side in range(2):
                ways = [way for way in (-1, 1) if (way, k - 1, side, 0) in moved]
                for half in range(2):
                    for way in ways:
                        moved[way, k - 1, side, half].wait_recv()
                        if k < 4:
                            go(way, k, side, half)
                for way in ways:
                    cross(SLOT[way * k], side)
                if k == 1 and side == 1:
                    over.wait_recv()
                    cross(0, 1)
                if k < 4:
                    yield
        yield

    def whole(crossed, slots):
        for slot in slots:
            for side in range(2):
                crossed[slot, side].wait_recv()

    crossed = {}
    steps = gather(cen, crossed)
    next(steps)

    def encode(group, latents):
        slot, count = group
        rows = pl.ds(PLANE * slot, PLANE * count)
        lanes = lax.broadcasted_iota(jnp.int32, (PLANE * count, 128), 1)
        lanes_f = lanes.astype(F32)
        picked = jnp.zeros((PLANE * count, 128), F32) if latents[0] == 0 else vals[rows, :]
        for j in latents:
            pre = jnp.dot(
                cen[rows, :], ew_v[:, STRIDE * j:STRIDE * (j + 1)], preferred_element_type=F32
            )
            where = off[j, rows, :]
            total = jnp.zeros((PLANE * count, 128), F32)
            for q in range(4):
                total += jnp.where(lanes_f + 128.0 * q == where, pre[:, 128 * q:128 * (q + 1)], 0.0)
            picked += jnp.where(lanes == j, jnp.sum(total, axis=1, keepdims=True), 0.0)
        vals[rows, :] = picked

    def pack(slots):
        for slot in slots:
            rows = pl.ds(PLANE * slot, PLANE)
            packed[0, :, rows] = vals[rows, :].T[:8, :]
        lanes = pl.ds(PLANE * slots[0], PLANE * len(slots))
        for k in range(1, HEADS):
            arrived[slots[0], k] = send(
                packed.at[0, :, lanes], packed.at[k, :, lanes], {"head": heads[k]}
            )

    arrived = {}
    loads[4].wait()
    for n in range(3):
        slot, count = GROUPS[n]
        next(steps)
        if n:
            whole(crossed, range(slot, slot + count))
            encode(GROUPS[n], (0, 1))
        next(steps)
        if n:
            encode(GROUPS[n], (2, 3))
        else:
            whole(crossed, (0,))
            encode(GROUPS[0], (0, 1, 2, 3))
    next(steps)
    pack(range(0, 5))
    whole(crossed, (5, 6))
    encode(GROUPS[3], (0, 1, 2, 3))
    pack((5, 6))
    whole(crossed, (7,))
    encode(GROUPS[4], (0, 1, 2, 3))
    pack((7,))

    loads[5].wait()
    crossed_sums = {}

    def decode(group):
        slot, count = group

        def fill(i, carry):
            rows = pl.ds(pl.multiple_of(PLANE * (slot + i), PLANE), PLANE)
            total = packed[0, :, rows]
            for k in range(1, HEADS):
                total += packed[k, :, rows]
            value = jnp.concatenate([total, jnp.zeros((PLANE - 8, PLANE), F32)], axis=0).T
            value = jnp.maximum(value + biases[rows, :], 0.0)
            for j in range(HERE):
                column = jnp.broadcast_to(value[:, j:j + 1], (PLANE, 128))
                where = off[j, rows, :]
                for q in range(4):
                    lat[pl.ds(pl.multiple_of(PLANE * i, PLANE), PLANE),
                        STRIDE * j + 128 * q:STRIDE * j + 128 * (q + 1)] = jnp.where(
                            lane_f + 128.0 * q == where, column, 0.0).astype(BF16)
            return carry

        lax.fori_loop(0, count, fill, 0)

        def body(n, carry):
            cols = pl.ds(pl.multiple_of(n * 512, 512), 512)
            total = jnp.dot(lat[pl.ds(0, PLANE * count), :], dw_v[:, cols], preferred_element_type=F32)
            for i in range(count):
                own_part[slot + i, :, cols] = total[PLANE * i:PLANE * i + 64]
                core_out[slot + i, :, cols] = total[PLANE * i + 64:PLANE * (i + 1)].astype(BF16)
            return carry

        lax.fori_loop(0, WIDTH // 512, body, 0, unroll=True)
        for i in range(count):
            crossed_sums[slot + i] = send(core_out.at[slot + i], core_in.at[slot + i], cn)

    def summed(slot, side):
        rows = pl.ds(BLOCK * side, BLOCK)
        return own_part[slot, rows, :] + core_in[slot, rows, :].astype(F32)

    plus, minus = {}, {}

    def ring(out, arrived_at, table, target, n, slot, side):
        total = summed(slot, side)
        if n > 1:
            table[n - 2].wait_recv()
            total += arrived_at[n - 2].astype(F32)
        out[n] = total.astype(BF16)
        table[n] = send(out.at[n], arrived_at.at[n], target)

    def ring_step(k):
        for n, side in ((6 - 2 * k, 1), (7 - 2 * k, 0)):
            diagonal = k == 1 and side == 1
            ring(zp_out, zp_in, plus, zp_other if diagonal else zp, n, SLOT[k], side)
            ring(zm_out, zm_in, minus, zm_other if diagonal else zm, n, SLOT[-k], side)

    def get(slot):
        for k in range(1, HEADS):
            arrived[slot, k].wait_recv()

    def meet(*slots):
        for slot in slots:
            crossed_sums[slot].wait_recv()

    get(5)
    decode((5, 2))
    get(7)
    decode((7, 1))
    meet(5, 6)
    ring_step(3)
    meet(7)
    x_out[0] = summed(7, 1).astype(BF16)
    x_far = send(x_out.at[0], x_in.at[0], xn)
    get(0)
    decode((3, 2))
    decode((1, 2))
    decode((0, 1))
    meet(3, 4)
    ring_step(2)
    x_far.wait_recv()
    x_out[1] = (summed(7, 0) + x_in[0].astype(F32)).astype(BF16)
    x_far = send(x_out.at[1], x_in.at[1], far)
    meet(0)
    x_out[2] = summed(0, 1).astype(BF16)
    x_near = send(x_out.at[2], x_in.at[2], xn)
    meet(1, 2)
    ring_step(1)
    mine = summed(0, 0) + db_v[...]
    x_near.wait_recv()
    x_far.wait_recv()
    mine += x_in[1].astype(F32) + x_in[2].astype(F32)
    for n in (4, 5):
        plus[n].wait_recv()
        minus[n].wait_recv()
        mine += zp_in[n].astype(F32) + zm_in[n].astype(F32)
    rec[pl.ds(0, BLOCK), :] = mine.astype(BF16)

    crossed = {}
    steps = gather(rec, crossed)
    next(steps)
    store_rec = pltpu.make_async_copy(rec.at[pl.ds(0, BLOCK), :], rec_out, store_sem.at[0])
    store_rec.start()
    loads[6].wait()
    spread = {}

    def project(group):
        slot, count = group
        out = jnp.dot(
            rec[pl.ds(PLANE * slot, PLANE * count), :], ow_v[...], preferred_element_type=F32
        ).astype(BF16)
        for i in range(count):
            part[slot + i] = out[PLANE * i:PLANE * (i + 1)]
        for k in range(1, HEADS):
            rows = pl.ds(pl.multiple_of(heads[k] * 16, 16), 16)
            spread[slot, k] = send(
                part.at[pl.ds(slot, count), rows, :],
                part_in.at[k, pl.ds(slot, count)],
                {"head": heads[k]},
            )

    def finish(group):
        slot, count = group
        for k in range(1, HEADS):
            spread[slot, k].wait_recv()
        rows = pl.ds(pl.multiple_of(h * 16, 16), 16)
        for s in range(slot, slot + count):
            total = part[s, rows, :].astype(F32)
            for k in range(1, HEADS):
                total += part_in[k, s].astype(F32)
            piece[s] = total.astype(BF16)
            n = len(sent)
            sent.append(None)
            copy = pltpu.make_async_remote_copy(
                src_ref=piece.at[s],
                dst_ref=piece_in.at[t % 4, h % 2],
                send_sem=send_sem.at[n],
                recv_sem=last_recv.at[t % 4, h % 2],
                device_id={"head": out_head, "tok": final_tok[s]},
                device_id_type=MESH,
            )
            if s:
                copy.start()
                sent[n] = copy
                continue
            local = pltpu.make_async_copy(piece.at[0], piece_in.at[t % 4, h % 2], last_recv.at[t % 4, h % 2])

            @pl.when(to_self)
            def _():
                local.start()

            @pl.when(jnp.logical_not(to_self))
            def _():
                copy.start()

            own_piece.append(copy)

    own_piece = []
    for n in range(3):
        slot, count = GROUPS[n]
        next(steps)
        next(steps)
        whole(crossed, range(slot, slot + count))
        project(GROUPS[n])
        if n:
            finish(GROUPS[n - 1])
    next(steps)
    whole(crossed, (5, 6))
    project(GROUPS[3])
    whole(crossed, (7,))
    project(GROUPS[4])
    for n in range(2, 5):
        finish(GROUPS[n])
    for copy in sent:
        if copy is not None:
            copy.wait_send()

    @pl.when(jnp.logical_not(to_self))
    def _():
        own_piece[0].wait_send()

    store_rec.wait()
    for j in range(4):
        for half in range(2):
            pltpu.make_async_copy(piece_in.at[j, half], piece_in.at[j, half], last_recv.at[j, half]).wait()
            proj_v[16 * half:16 * half + 16, COLS * j:COLS * (j + 1)] = piece_in[j, half]
    store_proj = pltpu.make_async_copy(proj_v, proj_out, store_sem.at[1])
    store_proj.start()
    store_proj.wait()


def on_device(head_outputs, dec_bias, enc_bias, enc_weight, dec_weight, out_weight, active_ids):
    block = jax.ShapeDtypeStruct((BLOCK, WIDTH), BF16)
    vmem = pltpu.VMEM
    return pl.pallas_call(
        kernel,
        out_shape=(block, block),
        in_specs=[pl.BlockSpec(memory_space=pl.ANY)] * 7,
        out_specs=(pl.BlockSpec(memory_space=pl.ANY),) * 2,
        scratch_shapes=[
            vmem((BLOCK, WIDTH), BF16),
            vmem((1, WIDTH), F32),
            vmem((1, LATS), F32),
            vmem((WIDTH, LATS), BF16),
            vmem((LATS, WIDTH), BF16),
            vmem((WIDTH, COLS), BF16),
            vmem((TOKENS, 128), jnp.int32),
            vmem((TOKENS, WIDTH), BF16),
            vmem((HERE, TOKENS, 128), F32),
            vmem((TOKENS, 128), F32),
            vmem((HEADS, 8, TOKENS), F32),
            vmem((2 * PLANE, LATS), BF16),
            vmem((8, 64, WIDTH), F32),
            vmem((8, 64, WIDTH), BF16),
            vmem((8, 64, WIDTH), BF16),
            vmem((6, BLOCK, WIDTH), BF16),
            vmem((6, BLOCK, WIDTH), BF16),
            vmem((6, BLOCK, WIDTH), BF16),
            vmem((6, BLOCK, WIDTH), BF16),
            vmem((3, BLOCK, WIDTH), BF16),
            vmem((3, BLOCK, WIDTH), BF16),
            vmem((TOKENS, WIDTH), BF16),
            vmem((TOKENS, 128), F32),
            vmem((8, PLANE, COLS), BF16),
            vmem((HEADS, 8, 16, COLS), BF16),
            vmem((8, 16, COLS), BF16),
            vmem((4, 2, 16, COLS), BF16),
            vmem((BLOCK, WIDTH), BF16),
            pltpu.SemaphoreType.DMA((7,)),
            pltpu.SemaphoreType.DMA((MESSAGES,)),
            pltpu.SemaphoreType.DMA((MESSAGES,)),
            pltpu.SemaphoreType.DMA((4, 2)),
            pltpu.SemaphoreType.DMA((2,)),
        ],
        compiler_params=pltpu.CompilerParams(
            collective_id=0, has_side_effects=True, vmem_limit_bytes=60 * 2 ** 20
        ),
        cost_estimate=pl.CostEstimate(flops=9 * 10 ** 9, bytes_accessed=9 * 2 ** 20, transcendentals=0),
    )(
        head_outputs,
        dec_bias.reshape(1, WIDTH),
        enc_bias.reshape(1, LATS),
        enc_weight,
        dec_weight,
        out_weight,
        active_ids,
    )


def solution(mesh):
    return jax.shard_map(
        on_device,
        mesh=mesh,
        in_specs=(
            P("tok", "head"),
            P("head"),
            P("tok"),
            P("head", "tok"),
            P("tok", "head"),
            P("head", "tok"),
            P(),
        ),
        out_specs=(P("tok", "head"), P("tok", "head")),
        check_vma=False,
    )
```

```python
import jax
import jax.numpy as jnp
from jax import lax
from jax.experimental import pallas as pl
from jax.experimental.pallas import tpu as pltpu
from jax.sharding import PartitionSpec as P

MESH = pl.DeviceIdType.MESH
F32, BF16 = jnp.float32, jnp.bfloat16

HEADS = 8
TOKENS, WIDTH, BLOCK = 1024, 1024, 32
LATS, HERE, STRIDE = 2048, 4, 512
COLS = 256
PLANE = 128
PLANES = (0, -1, 1, -2, 2, -3, 3, 4)
SLOT = {0: 0, -1: 1, 1: 2, -2: 3, 2: 4, -3: 5, 3: 6, -4: 7, 4: 7}
GROUPS = ((0, 1), (1, 2), (3, 2), (5, 2), (7, 1))
MESSAGES = 256


def row_of(slot, core, side):
    return PLANE * slot + 64 * core + BLOCK * side


def kernel(
    ho, dbias, ebias, ew, dw, ow, ids,
    rec_out, proj_out,
    ho_v, db_v, eb_v, ew_v, dw_v, ow_v, ids_v,
    cen, off, vals, packed, lat, own_part, core_out, core_in,
    zp_out, zp_in, zm_out, zm_in, x_out, x_in, rec, biases,
    part, part_in, piece, piece_in, proj_v,
    load_sem, send_sem, recv_sem, last_recv, store_sem,
):
    h = lax.axis_index("head")
    t = lax.axis_index("tok")
    core, z, side = t % 2, (t // 2) % 8, t // 16

    def tok_of(dside, dz, dcore):
        return ((side + dside) % 2) * 16 + ((z + dz) % 8) * 2 + (core + dcore) % 2

    zp, zm = {"tok": tok_of(0, 1, 0)}, {"tok": tok_of(0, 7, 0)}
    zp_other, zm_other = {"tok": tok_of(1, 1, 0)}, {"tok": tok_of(1, 7, 0)}
    xn, cn, far = {"tok": tok_of(1, 0, 0)}, {"tok": tok_of(0, 0, 1)}, {"tok": tok_of(0, 4, 0)}
    heads = [(h + k) % HEADS for k in range(HEADS)]
    out_head = t // 4
    my_part = h // 2
    final_tok = [tok_of(my_part % 2, PLANES[s] % 8, my_part // 2) for s in range(8)]
    to_self = (out_head == h) & (my_part == 0)

    loads = []
    for n, (src, dst) in enumerate(
        ((ho, ho_v), (dbias, db_v), (ids, ids_v), (ebias, eb_v), (ew, ew_v), (dw, dw_v), (ow, ow_v))
    ):
        loads.append(pltpu.make_async_copy(src, dst, load_sem.at[n]))
        loads[-1].start()

    barrier = pltpu.get_barrier_semaphore()
    for target in (zp, zm, zp_other, zm_other, xn, cn, far):
        pl.semaphore_signal(barrier, inc=1, device_id=target, device_id_type=MESH)
    for k in range(1, HEADS):
        pl.semaphore_signal(barrier, inc=1, device_id={"head": heads[k]}, device_id_type=MESH)
    for s in range(8):
        target = {"head": out_head, "tok": final_tok[s]}
        pl.semaphore_signal(barrier, inc=1, device_id=target, device_id_type=MESH)

    loads[0].wait()
    loads[1].wait()
    cen[pl.ds(0, BLOCK), :] = (ho_v[...].astype(F32) - db_v[...]).astype(BF16)

    lane = lax.broadcasted_iota(jnp.int32, (PLANE, 128), 1)
    lane_f = lane.astype(F32)

    def offsets(slot):
        def row(q):
            return pl.multiple_of(
                ((side + q % 2) % 2) * 512 + ((z + PLANES[slot] % 8) % 8) * 64 + ((core + q // 2) % 2) * BLOCK,
                BLOCK,
            )

        rows = pl.ds(PLANE * slot, PLANE)
        here = jnp.concatenate([ids_v[pl.ds(row(q), BLOCK), :] for q in range(4)], axis=0)
        here = (here - t * LATS).astype(F32)
        bias = jnp.zeros((PLANE, 128), F32)
        for j in range(HERE):
            column = jnp.sum(jnp.where(lane == t * HERE + j, here, 0.0), axis=1, keepdims=True) - j * STRIDE
            column = jnp.broadcast_to(column, (PLANE, 128))
            off[j, rows, :] = column
            total = jnp.zeros((PLANE, 128), F32)
            for q in range(4):
                first = STRIDE * j + 128 * q
                total += jnp.where(lane_f + 128.0 * q == column, eb_v[:, first:first + 128], 0.0)
            bias += jnp.where(lane == j, jnp.sum(total, axis=1, keepdims=True), 0.0)
        biases[rows, :] = bias

    loads[2].wait()
    loads[3].wait()
    for slot in range(8):
        offsets(slot)
    pl.semaphore_wait(barrier, 7 + 7 + 8)

    sent = []

    def send(src, dst, target):
        n = len(sent)
        copy = pltpu.make_async_remote_copy(
            src_ref=src, dst_ref=dst, send_sem=send_sem.at[n], recv_sem=recv_sem.at[n],
            device_id=target, device_id_type=MESH,
        )
        copy.start()
        sent.append(copy)
        return copy

    def gather(buf, crossed):
        def block(slot, core, side):
            return buf.at[pl.ds(row_of(slot, core, side), BLOCK), :]

        def cross(slot, side):
            crossed[slot, side] = send(block(slot, 0, side), block(slot, 1, side), cn)

        moved = {}

        def go(way, k, side, half):
            if k == 0:
                src = part(0, 0, half)
                target = ((zp, zp_other), (zm, zm_other))[way > 0][side]
            else:
                src = part(SLOT[way * k], side, half)
                target = (zp, zm)[way > 0]
            moved[way, k, side, half] = send(src, part(SLOT[way * (k + 1)], side, half), target)

        def part(slot, side, half):
            return buf.at[pl.ds(row_of(slot, 0, side) + 16 * half, 16), :]

        for side in range(2):
            for half in range(2):
                for way in (-1, 1):
                    go(way, 0, side, half)
        direct = send(block(0, 0, 0), block(7, 0, 0), far)
        over = send(block(0, 0, 0), block(0, 0, 1), xn)
        cross(0, 0)
        yield
        for k in range(1, 4):
            for side in range(2):
                for half in range(2):
                    for way in (-1, 1):
                        moved[way, k - 1, side, half].wait_recv()
                        if k < 3:
                            go(way, k, side, half)
                for way in (-1, 1):
                    cross(SLOT[way * k], side)
                if k == 1 and side == 1:
                    over.wait_recv()
                    cross(0, 1)
                    direct.wait_recv()
                    direct = send(block(7, 0, 0), block(7, 0, 1), xn)
                    cross(7, 0)
                if k == 3 and side == 0:
                    direct.wait_recv()
                    cross(7, 1)
                yield

    def whole(crossed, slots):
        for slot in slots:
            for side in range(2):
                crossed[slot, side].wait_recv()

    crossed = {}
    steps = gather(cen, crossed)
    next(steps)

    def encode(group, latents):
        slot, count = group
        rows = pl.ds(PLANE * slot, PLANE * count)
        lanes = lax.broadcasted_iota(jnp.int32, (PLANE * count, 128), 1)
        lanes_f = lanes.astype(F32)
        picked = jnp.zeros((PLANE * count, 128), F32) if latents[0] == 0 else vals[rows, :]
        for j in latents:
            pre = jnp.dot(
                cen[rows, :], ew_v[:, STRIDE * j:STRIDE * (j + 1)], preferred_element_type=F32
            )
            where = off[j, rows, :]
            total = jnp.zeros((PLANE * count, 128), F32)
            for q in range(4):
                total += jnp.where(lanes_f + 128.0 * q == where, pre[:, 128 * q:128 * (q + 1)], 0.0)
            picked += jnp.where(lanes == j, jnp.sum(total, axis=1, keepdims=True), 0.0)
        vals[rows, :] = picked

    def pack(slots):
        for slot in slots:
            rows = pl.ds(PLANE * slot, PLANE)
            packed[0, :, rows] = vals[rows, :].T[:8, :]
        lanes = pl.ds(PLANE * slots[0], PLANE * len(slots))
        for k in range(1, HEADS):
            arrived[slots[0], k] = send(
                packed.at[0, :, lanes], packed.at[k, :, lanes], {"head": heads[k]}
            )

    arrived = {}
    loads[4].wait()
    next(steps)
    next(steps)
    whole(crossed, (0,))
    encode(GROUPS[0], (0, 1, 2, 3))
    for n in (1, 2):
        slot, count = GROUPS[n]
        next(steps)
        whole(crossed, range(slot, slot + count))
        encode(GROUPS[n], (0, 1))
        next(steps)
        encode(GROUPS[n], (2, 3))
    pack(range(0, 5))
    whole(crossed, (7,))
    encode(GROUPS[4], (0, 1, 2, 3))
    pack((7,))
    whole(crossed, (5, 6))
    encode(GROUPS[3], (0, 1, 2, 3))
    pack((5, 6))

    loads[5].wait()
    crossed_sums = {}

    def decode(group):
        slot, count = group

        def fill(i, carry):
            rows = pl.ds(pl.multiple_of(PLANE * (slot + i), PLANE), PLANE)
            total = packed[0, :, rows]
            for k in range(1, HEADS):
                total += packed[k, :, rows]
            value = jnp.concatenate([total, jnp.zeros((PLANE - 8, PLANE), F32)], axis=0).T
            value = jnp.maximum(value + biases[rows, :], 0.0)
            for j in range(HERE):
                column = jnp.broadcast_to(value[:, j:j + 1], (PLANE, 128))
                where = off[j, rows, :]
                for q in range(4):
                    lat[pl.ds(pl.multiple_of(PLANE * i, PLANE), PLANE),
                        STRIDE * j + 128 * q:STRIDE * j + 128 * (q + 1)] = jnp.where(
                            lane_f + 128.0 * q == where, column, 0.0).astype(BF16)
            return carry

        lax.fori_loop(0, count, fill, 0)

        total = jnp.dot(lat[pl.ds(0, PLANE * count), :], dw_v[...], preferred_element_type=F32)
        for i in range(count):
            own_part[slot + i] = total[PLANE * i:PLANE * i + 64]
            core_out[slot + i] = total[PLANE * i + 64:PLANE * (i + 1)].astype(BF16)
        for i in range(count):
            crossed_sums[slot + i] = send(core_out.at[slot + i], core_in.at[slot + i], cn)

    def summed(slot, side):
        rows = pl.ds(BLOCK * side, BLOCK)
        return own_part[slot, rows, :] + core_in[slot, rows, :].astype(F32)

    plus, minus = {}, {}

    def ring(out, arrived_at, table, target, n, slot, piece):
        rows = pl.ds(16 * piece, 16)
        total = own_part[slot, rows, :] + core_in[slot, rows, :].astype(F32)
        if n > 3:
            table[n - 4].wait_recv()
            total += arrived_at[n - 4].astype(F32)
        out[n] = total.astype(BF16)
        table[n] = send(out.at[n], arrived_at.at[n], target)

    def ring_step(k):
        for i, piece in enumerate((2, 3, 0, 1)):
            diagonal = k == 1 and piece > 1
            n = 4 * (3 - k) + i
            ring(zp_out, zp_in, plus, zp_other if diagonal else zp, n, SLOT[k], piece)
            ring(zm_out, zm_in, minus, zm_other if diagonal else zm, n, SLOT[-k], piece)

    def get(slot):
        for k in range(1, HEADS):
            arrived[slot, k].wait_recv()

    def meet(*slots):
        for slot in slots:
            crossed_sums[slot].wait_recv()

    get(7)
    decode((7, 1))
    get(0)
    decode((3, 2))
    meet(7)
    x_out[0] = summed(7, 1).astype(BF16)
    x_far = send(x_out.at[0], x_in.at[0], xn)
    get(5)
    decode((5, 2))
    decode((0, 1))
    meet(5, 6)
    ring_step(3)
    decode((1, 2))
    x_far.wait_recv()
    x_out[1] = (summed(7, 0) + x_in[0].astype(F32)).astype(BF16)
    x_far = send(x_out.at[1], x_in.at[1], far)
    meet(0)
    x_out[2] = summed(0, 1).astype(BF16)
    x_near = send(x_out.at[2], x_in.at[2], xn)
    meet(3, 4)
    ring_step(2)
    meet(1, 2)
    ring_step(1)
    mine = summed(0, 0) + db_v[...]
    x_near.wait_recv()
    x_far.wait_recv()
    mine += x_in[1].astype(F32) + x_in[2].astype(F32)
    for half in range(2):
        rows = slice(16 * half, 16 * half + 16)
        total = mine[rows]
        for n in (8 + half, 10 + half):
            plus[n].wait_recv()
            minus[n].wait_recv()
            total += zp_in[n].astype(F32) + zm_in[n].astype(F32)
        rec[rows, :] = total.astype(BF16)

    crossed = {}
    steps = gather(rec, crossed)
    next(steps)
    store_rec = pltpu.make_async_copy(rec.at[pl.ds(0, BLOCK), :], rec_out, store_sem.at[0])
    store_rec.start()
    loads[6].wait()
    spread = {}

    def project(group):
        slot, count = group
        out = jnp.dot(
            rec[pl.ds(PLANE * slot, PLANE * count), :], ow_v[...], preferred_element_type=F32
        ).astype(BF16)
        for i in range(count):
            part[slot + i] = out[PLANE * i:PLANE * (i + 1)]
        for k in range(1, HEADS):
            rows = pl.ds(pl.multiple_of(heads[k] * 16, 16), 16)
            spread[slot, k] = send(
                part.at[pl.ds(slot, count), rows, :],
                part_in.at[k, pl.ds(slot, count)],
                {"head": heads[k]},
            )

    def finish(group):
        slot, count = group
        for k in range(1, HEADS):
            spread[slot, k].wait_recv()
        rows = pl.ds(pl.multiple_of(h * 16, 16), 16)
        for s in range(slot, slot + count):
            total = part[s, rows, :].astype(F32)
            for k in range(1, HEADS):
                total += part_in[k, s].astype(F32)
            piece[s] = total.astype(BF16)
            n = len(sent)
            sent.append(None)
            copy = pltpu.make_async_remote_copy(
                src_ref=piece.at[s],
                dst_ref=piece_in.at[t % 4, h % 2],
                send_sem=send_sem.at[n],
                recv_sem=last_recv.at[t % 4, h % 2],
                device_id={"head": out_head, "tok": final_tok[s]},
                device_id_type=MESH,
            )
            if s:
                copy.start()
                sent[n] = copy
                continue
            local = pltpu.make_async_copy(piece.at[0], piece_in.at[t % 4, h % 2], last_recv.at[t % 4, h % 2])

            @pl.when(to_self)
            def _():
                local.start()

            @pl.when(jnp.logical_not(to_self))
            def _():
                copy.start()

            own_piece.append(copy)

    own_piece = []
    next(steps)
    next(steps)
    whole(crossed, (0,))
    project(GROUPS[0])
    next(steps)
    whole(crossed, (1, 2))
    project(GROUPS[1])
    next(steps)
    finish(GROUPS[0])
    next(steps)
    whole(crossed, (3, 4))
    project(GROUPS[2])
    next(steps)
    finish(GROUPS[1])
    whole(crossed, (7,))
    project(GROUPS[4])
    whole(crossed, (5, 6))
    project(GROUPS[3])
    finish(GROUPS[2])
    finish(GROUPS[4])
    finish(GROUPS[3])
    for copy in sent:
        if copy is not None:
            copy.wait_send()

    @pl.when(jnp.logical_not(to_self))
    def _():
        own_piece[0].wait_send()

    store_rec.wait()
    for j in range(4):
        for half in range(2):
            pltpu.make_async_copy(piece_in.at[j, half], piece_in.at[j, half], last_recv.at[j, half]).wait()
            proj_v[16 * half:16 * half + 16, COLS * j:COLS * (j + 1)] = piece_in[j, half]
    store_proj = pltpu.make_async_copy(proj_v, proj_out, store_sem.at[1])
    store_proj.start()
    store_proj.wait()


def hand_over(rec_in, proj_in, rec_out, proj_out, sem):
    copies = [
        pltpu.make_async_copy(rec_in, rec_out, sem.at[0]),
        pltpu.make_async_copy(proj_in, proj_out, sem.at[1]),
    ]
    for copy in copies:
        copy.start()
    for copy in copies:
        copy.wait()


def on_device(head_outputs, dec_bias, enc_bias, enc_weight, dec_weight, out_weight, active_ids):
    block = jax.ShapeDtypeStruct((BLOCK, WIDTH), BF16)
    vmem = pltpu.VMEM
    results = pl.pallas_call(
        kernel,
        out_shape=(block, block),
        in_specs=[pl.BlockSpec(memory_space=pl.ANY)] * 7,
        out_specs=(pl.BlockSpec(memory_space=pl.ANY),) * 2,
        scratch_shapes=[
            vmem((BLOCK, WIDTH), BF16),
            vmem((1, WIDTH), F32),
            vmem((1, LATS), F32),
            vmem((WIDTH, LATS), BF16),
            vmem((LATS, WIDTH), BF16),
            vmem((WIDTH, COLS), BF16),
            vmem((TOKENS, 128), jnp.int32),
            vmem((TOKENS, WIDTH), BF16),
            vmem((HERE, TOKENS, 128), F32),
            vmem((TOKENS, 128), F32),
            vmem((HEADS, 8, TOKENS), F32),
            vmem((2 * PLANE, LATS), BF16),
            vmem((8, 64, WIDTH), F32),
            vmem((8, 64, WIDTH), BF16),
            vmem((8, 64, WIDTH), BF16),
            vmem((12, 16, WIDTH), BF16),
            vmem((12, 16, WIDTH), BF16),
            vmem((12, 16, WIDTH), BF16),
            vmem((12, 16, WIDTH), BF16),
            vmem((3, BLOCK, WIDTH), BF16),
            vmem((3, BLOCK, WIDTH), BF16),
            vmem((TOKENS, WIDTH), BF16),
            vmem((TOKENS, 128), F32),
            vmem((8, PLANE, COLS), BF16),
            vmem((HEADS, 8, 16, COLS), BF16),
            vmem((8, 16, COLS), BF16),
            vmem((4, 2, 16, COLS), BF16),
            vmem((BLOCK, WIDTH), BF16),
            pltpu.SemaphoreType.DMA((7,)),
            pltpu.SemaphoreType.DMA((MESSAGES,)),
            pltpu.SemaphoreType.DMA((MESSAGES,)),
            pltpu.SemaphoreType.DMA((4, 2)),
            pltpu.SemaphoreType.DMA((2,)),
        ],
        compiler_params=pltpu.CompilerParams(
            collective_id=0, has_side_effects=True, vmem_limit_bytes=60 * 2 ** 20
        ),
        cost_estimate=pl.CostEstimate(flops=9 * 10 ** 9, bytes_accessed=9 * 2 ** 20, transcendentals=0),
    )(
        head_outputs,
        dec_bias.reshape(1, WIDTH),
        enc_bias.reshape(1, LATS),
        enc_weight,
        dec_weight,
        out_weight,
        active_ids,
    )
    return pl.pallas_call(
        hand_over,
        out_shape=(block, block),
        in_specs=[pl.BlockSpec(memory_space=pl.ANY)] * 2,
        out_specs=(pl.BlockSpec(memory_space=pl.ANY),) * 2,
        scratch_shapes=[pltpu.SemaphoreType.DMA((2,))],
    )(*results)


def solution(mesh):
    return jax.shard_map(
        on_device,
        mesh=mesh,
        in_specs=(
            P("tok", "head"),
            P("head"),
            P("tok"),
            P("head", "tok"),
            P("tok", "head"),
            P("head", "tok"),
            P(),
        ),
        out_specs=(P("tok", "head"), P("tok", "head")),
        check_vma=False,
    )
```

```python
import jax
import jax.numpy as jnp
from jax import lax
from jax.experimental import pallas as pl
from jax.experimental.pallas import tpu as pltpu
from jax.sharding import PartitionSpec as P

MESH = pl.DeviceIdType.MESH
F32, BF16 = jnp.float32, jnp.bfloat16

HEADS = 8
TOKENS, WIDTH, BLOCK = 1024, 1024, 32
LATS, HERE, STRIDE = 2048, 4, 512
COLS = 256
PLANE = 128
PLANES = (0, -1, 1, -2, 2, -3, 3, 4)
SLOT = {0: 0, -1: 1, 1: 2, -2: 3, 2: 4, -3: 5, 3: 6, -4: 7, 4: 7}
GROUPS = ((0, 1), (1, 2), (3, 2), (5, 2), (7, 1))
MESSAGES = 256


def row_of(slot, core, side):
    return PLANE * slot + 64 * core + BLOCK * side


def kernel(
    ho, dbias, ebias, ew, dw, ow, ids,
    both_out,
    ho_v, db_v, eb_v, ew_v, dw_v, ow_v, ids_v,
    cen, off, vals, packed, lat, own_part, core_out, core_in,
    zp_out, zp_in, zm_out, zm_in, x_out, x_in, rec, biases,
    part, part_in, piece, piece_in, proj_v,
    load_sem, send_sem, recv_sem, last_recv, store_sem,
):
    h = lax.axis_index("head")
    t = lax.axis_index("tok")
    core, z, side = t % 2, (t // 2) % 8, t // 16

    def tok_of(dside, dz, dcore):
        return ((side + dside) % 2) * 16 + ((z + dz) % 8) * 2 + (core + dcore) % 2

    zp, zm = {"tok": tok_of(0, 1, 0)}, {"tok": tok_of(0, 7, 0)}
    zp_other, zm_other = {"tok": tok_of(1, 1, 0)}, {"tok": tok_of(1, 7, 0)}
    xn, cn, far = {"tok": tok_of(1, 0, 0)}, {"tok": tok_of(0, 0, 1)}, {"tok": tok_of(0, 4, 0)}
    heads = [(h + k) % HEADS for k in range(HEADS)]
    out_head = t // 4
    my_part = h // 2
    final_tok = [tok_of(my_part % 2, PLANES[s] % 8, my_part // 2) for s in range(8)]
    to_self = (out_head == h) & (my_part == 0)

    loads = []
    for n, (src, dst) in enumerate(
        ((ho, ho_v), (dbias, db_v), (ids, ids_v), (ebias, eb_v), (ew, ew_v), (dw, dw_v), (ow, ow_v))
    ):
        loads.append(pltpu.make_async_copy(src, dst, load_sem.at[n]))
        loads[-1].start()

    barrier = pltpu.get_barrier_semaphore()
    for target in (zp, zm, zp_other, zm_other, xn, cn, far):
        pl.semaphore_signal(barrier, inc=1, device_id=target, device_id_type=MESH)
    for k in range(1, HEADS):
        pl.semaphore_signal(barrier, inc=1, device_id={"head": heads[k]}, device_id_type=MESH)
    for s in range(8):
        target = {"head": out_head, "tok": final_tok[s]}
        pl.semaphore_signal(barrier, inc=1, device_id=target, device_id_type=MESH)

    loads[0].wait()
    loads[1].wait()
    cen[pl.ds(0, BLOCK), :] = (ho_v[...].astype(F32) - db_v[...]).astype(BF16)

    lane = lax.broadcasted_iota(jnp.int32, (PLANE, 128), 1)
    lane_f = lane.astype(F32)

    def offsets(slot):
        def row(q):
            return pl.multiple_of(
                ((side + q % 2) % 2) * 512 + ((z + PLANES[slot] % 8) % 8) * 64 + ((core + q // 2) % 2) * BLOCK,
                BLOCK,
            )

        rows = pl.ds(PLANE * slot, PLANE)
        here = jnp.concatenate([ids_v[pl.ds(row(q), BLOCK), :] for q in range(4)], axis=0)
        here = (here - t * LATS).astype(F32)
        bias = jnp.zeros((PLANE, 128), F32)
        for j in range(HERE):
            column = jnp.sum(jnp.where(lane == t * HERE + j, here, 0.0), axis=1, keepdims=True) - j * STRIDE
            column = jnp.broadcast_to(column, (PLANE, 128))
            off[j, rows, :] = column
            total = jnp.zeros((PLANE, 128), F32)
            for q in range(4):
                first = STRIDE * j + 128 * q
                total += jnp.where(lane_f + 128.0 * q == column, eb_v[:, first:first + 128], 0.0)
            bias += jnp.where(lane == j, jnp.sum(total, axis=1, keepdims=True), 0.0)
        biases[rows, :] = bias

    loads[2].wait()
    loads[3].wait()
    for slot in range(8):
        offsets(slot)
    pl.semaphore_wait(barrier, 7 + 7 + 8)

    sent = []

    def send(src, dst, target):
        n = len(sent)
        copy = pltpu.make_async_remote_copy(
            src_ref=src, dst_ref=dst, send_sem=send_sem.at[n], recv_sem=recv_sem.at[n],
            device_id=target, device_id_type=MESH,
        )
        copy.start()
        sent.append(copy)
        return copy

    def gather(buf, crossed):
        def block(slot, core, side):
            return buf.at[pl.ds(row_of(slot, core, side), BLOCK), :]

        def cross(slot, side):
            crossed[slot, side] = send(block(slot, 0, side), block(slot, 1, side), cn)

        moved = {}

        def go(way, k, side, half):
            if k == 0:
                src = part(0, 0, half)
                target = ((zp, zp_other), (zm, zm_other))[way > 0][side]
            else:
                src = part(SLOT[way * k], side, half)
                target = (zp, zm)[way > 0]
            moved[way, k, side, half] = send(src, part(SLOT[way * (k + 1)], side, half), target)

        def part(slot, side, half):
            return buf.at[pl.ds(row_of(slot, 0, side) + 16 * half, 16), :]

        for side in range(2):
            for half in range(2):
                for way in (-1, 1):
                    go(way, 0, side, half)
        direct = send(block(0, 0, 0), block(7, 0, 0), far)
        over = send(block(0, 0, 0), block(0, 0, 1), xn)
        cross(0, 0)
        yield
        for k in range(1, 4):
            for side in range(2):
                for half in range(2):
                    for way in (-1, 1):
                        moved[way, k - 1, side, half].wait_recv()
                        if k < 3:
                            go(way, k, side, half)
                for way in (-1, 1):
                    cross(SLOT[way * k], side)
                if k == 1 and side == 1:
                    over.wait_recv()
                    cross(0, 1)
                    direct.wait_recv()
                    direct = send(block(7, 0, 0), block(7, 0, 1), xn)
                    cross(7, 0)
                if k == 3 and side == 0:
                    direct.wait_recv()
                    cross(7, 1)
                yield

    def whole(crossed, slots):
        for slot in slots:
            for side in range(2):
                crossed[slot, side].wait_recv()

    crossed = {}
    steps = gather(cen, crossed)
    next(steps)

    def encode(group, latents):
        slot, count = group
        rows = pl.ds(PLANE * slot, PLANE * count)
        lanes = lax.broadcasted_iota(jnp.int32, (PLANE * count, 128), 1)
        lanes_f = lanes.astype(F32)
        picked = jnp.zeros((PLANE * count, 128), F32) if latents[0] == 0 else vals[rows, :]
        for j in latents:
            pre = jnp.dot(
                cen[rows, :], ew_v[:, STRIDE * j:STRIDE * (j + 1)], preferred_element_type=F32
            )
            where = off[j, rows, :]
            total = jnp.zeros((PLANE * count, 128), F32)
            for q in range(4):
                total += jnp.where(lanes_f + 128.0 * q == where, pre[:, 128 * q:128 * (q + 1)], 0.0)
            picked += jnp.where(lanes == j, jnp.sum(total, axis=1, keepdims=True), 0.0)
        vals[rows, :] = picked

    def pack(slots):
        for slot in slots:
            rows = pl.ds(PLANE * slot, PLANE)
            packed[0, :, rows] = vals[rows, :].T[:8, :]
        lanes = pl.ds(PLANE * slots[0], PLANE * len(slots))
        for k in range(1, HEADS):
            arrived[slots[0], k] = send(
                packed.at[0, :, lanes], packed.at[k, :, lanes], {"head": heads[k]}
            )

    arrived = {}
    loads[4].wait()
    next(steps)
    next(steps)
    whole(crossed, (0,))
    encode(GROUPS[0], (0, 1, 2, 3))
    for n in (1, 2):
        slot, count = GROUPS[n]
        next(steps)
        whole(crossed, range(slot, slot + count))
        encode(GROUPS[n], (0, 1))
        next(steps)
        encode(GROUPS[n], (2, 3))
        if n == 1:
            pack((0, 1, 2))
    whole(crossed, (5, 6))
    encode(GROUPS[3], (0, 1, 2, 3))
    pack((5, 6))
    whole(crossed, (7,))
    encode(GROUPS[4], (0, 1, 2, 3))
    pack((7,))
    pack((3, 4))

    loads[5].wait()
    crossed_sums = {}

    def decode(group):
        slot, count = group

        def fill(i, carry):
            rows = pl.ds(pl.multiple_of(PLANE * (slot + i), PLANE), PLANE)
            total = packed[0, :, rows]
            for k in range(1, HEADS):
                total += packed[k, :, rows]
            value = jnp.concatenate([total, jnp.zeros((PLANE - 8, PLANE), F32)], axis=0).T
            value = jnp.maximum(value + biases[rows, :], 0.0)
            for j in range(HERE):
                column = jnp.broadcast_to(value[:, j:j + 1], (PLANE, 128))
                where = off[j, rows, :]
                for q in range(4):
                    lat[pl.ds(pl.multiple_of(PLANE * i, PLANE), PLANE),
                        STRIDE * j + 128 * q:STRIDE * j + 128 * (q + 1)] = jnp.where(
                            lane_f + 128.0 * q == where, column, 0.0).astype(BF16)
            return carry

        lax.fori_loop(0, count, fill, 0)

        total = jnp.dot(lat[pl.ds(0, PLANE * count), :], dw_v[...], preferred_element_type=F32)
        for i in range(count):
            own_part[slot + i] = total[PLANE * i:PLANE * i + 64]
            core_out[slot + i] = total[PLANE * i + 64:PLANE * (i + 1)].astype(BF16)
        for i in range(count):
            crossed_sums[slot + i] = send(core_out.at[slot + i], core_in.at[slot + i], cn)

    def summed(slot, side):
        rows = pl.ds(BLOCK * side, BLOCK)
        return own_part[slot, rows, :] + core_in[slot, rows, :].astype(F32)

    plus, minus = {}, {}

    def ring(out, arrived_at, table, target, n, slot, piece):
        rows = pl.ds(16 * piece, 16)
        total = own_part[slot, rows, :] + core_in[slot, rows, :].astype(F32)
        if n > 3:
            table[n - 4].wait_recv()
            total += arrived_at[n - 4].astype(F32)
        out[n] = total.astype(BF16)
        table[n] = send(out.at[n], arrived_at.at[n], target)

    def ring_step(k):
        for i, piece in enumerate((2, 3, 0, 1)):
            diagonal = k == 1 and piece > 1
            n = 4 * (3 - k) + i
            ring(zp_out, zp_in, plus, zp_other if diagonal else zp, n, SLOT[k], piece)
            ring(zm_out, zm_in, minus, zm_other if diagonal else zm, n, SLOT[-k], piece)

    def get(slot):
        for k in range(1, HEADS):
            arrived[slot, k].wait_recv()

    def meet(*slots):
        for slot in slots:
            crossed_sums[slot].wait_recv()

    get(0)
    decode((0, 1))
    get(5)
    decode((5, 2))
    get(7)
    decode((7, 1))
    meet(5, 6)
    ring_step(3)
    meet(7)
    x_out[0] = summed(7, 1).astype(BF16)
    x_far = send(x_out.at[0], x_in.at[0], xn)
    meet(0)
    x_out[2] = summed(0, 1).astype(BF16)
    x_near = send(x_out.at[2], x_in.at[2], xn)
    get(3)
    decode((3, 2))
    decode((1, 2))
    x_far.wait_recv()
    x_out[1] = (summed(7, 0) + x_in[0].astype(F32)).astype(BF16)
    x_far = send(x_out.at[1], x_in.at[1], far)
    meet(3, 4)
    ring_step(2)
    meet(1, 2)
    ring_step(1)
    mine = summed(0, 0) + db_v[...]
    x_near.wait_recv()
    x_far.wait_recv()
    mine += x_in[1].astype(F32) + x_in[2].astype(F32)
    for half in range(2):
        rows = slice(16 * half, 16 * half + 16)
        total = mine[rows]
        for n in (8 + half, 10 + half):
            plus[n].wait_recv()
            minus[n].wait_recv()
            total += zp_in[n].astype(F32) + zm_in[n].astype(F32)
        rec[rows, :] = total.astype(BF16)

    crossed = {}
    steps = gather(rec, crossed)
    next(steps)
    store_rec = pltpu.make_async_copy(rec.at[pl.ds(0, BLOCK), :], both_out.at[0], store_sem.at[0])
    store_rec.start()
    loads[6].wait()
    spread = {}

    def project(group):
        slot, count = group
        out = jnp.dot(
            rec[pl.ds(PLANE * slot, PLANE * count), :], ow_v[...], preferred_element_type=F32
        ).astype(BF16)
        for i in range(count):
            part[slot + i] = out[PLANE * i:PLANE * (i + 1)]
        for k in range(1, HEADS):
            rows = pl.ds(pl.multiple_of(heads[k] * 16, 16), 16)
            spread[slot, k] = send(
                part.at[pl.ds(slot, count), rows, :],
                part_in.at[k, pl.ds(slot, count)],
                {"head": heads[k]},
            )

    def finish(group):
        slot, count = group
        for k in range(1, HEADS):
            spread[slot, k].wait_recv()
        rows = pl.ds(pl.multiple_of(h * 16, 16), 16)
        for s in range(slot, slot + count):
            total = part[s, rows, :].astype(F32)
            for k in range(1, HEADS):
                total += part_in[k, s].astype(F32)
            piece[s] = total.astype(BF16)
            n = len(sent)
            sent.append(None)
            copy = pltpu.make_async_remote_copy(
                src_ref=piece.at[s],
                dst_ref=piece_in.at[t % 4, h % 2],
                send_sem=send_sem.at[n],
                recv_sem=last_recv.at[t % 4, h % 2],
                device_id={"head": out_head, "tok": final_tok[s]},
                device_id_type=MESH,
            )
            if s:
                copy.start()
                sent[n] = copy
                continue
            local = pltpu.make_async_copy(piece.at[0], piece_in.at[t % 4, h % 2], last_recv.at[t % 4, h % 2])

            @pl.when(to_self)
            def _():
                local.start()

            @pl.when(jnp.logical_not(to_self))
            def _():
                copy.start()

            own_piece.append(copy)

    own_piece = []
    next(steps)
    next(steps)
    whole(crossed, (0,))
    project(GROUPS[0])
    next(steps)
    whole(crossed, (1, 2))
    project(GROUPS[1])
    next(steps)
    finish(GROUPS[0])
    next(steps)
    whole(crossed, (3, 4))
    project(GROUPS[2])
    next(steps)
    whole(crossed, (7,))
    project(GROUPS[4])
    whole(crossed, (5, 6))
    project(GROUPS[3])
    finish(GROUPS[1])
    finish(GROUPS[2])
    finish(GROUPS[4])
    finish(GROUPS[3])
    for copy in sent:
        if copy is not None:
            copy.wait_send()

    @pl.when(jnp.logical_not(to_self))
    def _():
        own_piece[0].wait_send()

    store_rec.wait()
    for j in range(4):
        for half in range(2):
            pltpu.make_async_copy(piece_in.at[j, half], piece_in.at[j, half], last_recv.at[j, half]).wait()
            proj_v[16 * half:16 * half + 16, COLS * j:COLS * (j + 1)] = piece_in[j, half]
    store_proj = pltpu.make_async_copy(proj_v, both_out.at[1], store_sem.at[1])
    store_proj.start()
    store_proj.wait()


def on_device(head_outputs, dec_bias, enc_bias, enc_weight, dec_weight, out_weight, active_ids):
    block = jax.ShapeDtypeStruct((BLOCK, WIDTH), BF16)
    vmem = pltpu.VMEM
    results = pl.pallas_call(
        kernel,
        out_shape=jax.ShapeDtypeStruct((2, BLOCK, WIDTH), BF16),
        in_specs=[pl.BlockSpec(memory_space=pl.ANY)] * 7,
        out_specs=pl.BlockSpec(memory_space=pl.ANY),
        scratch_shapes=[
            vmem((BLOCK, WIDTH), BF16),
            vmem((1, WIDTH), F32),
            vmem((1, LATS), F32),
            vmem((WIDTH, LATS), BF16),
            vmem((LATS, WIDTH), BF16),
            vmem((WIDTH, COLS), BF16),
            vmem((TOKENS, 128), jnp.int32),
            vmem((TOKENS, WIDTH), BF16),
            vmem((HERE, TOKENS, 128), F32),
            vmem((TOKENS, 128), F32),
            vmem((HEADS, 8, TOKENS), F32),
            vmem((2 * PLANE, LATS), BF16),
            vmem((8, 64, WIDTH), F32),
            vmem((8, 64, WIDTH), BF16),
            vmem((8, 64, WIDTH), BF16),
            vmem((12, 16, WIDTH), BF16),
            vmem((12, 16, WIDTH), BF16),
            vmem((12, 16, WIDTH), BF16),
            vmem((12, 16, WIDTH), BF16),
            vmem((3, BLOCK, WIDTH), BF16),
            vmem((3, BLOCK, WIDTH), BF16),
            vmem((TOKENS, WIDTH), BF16),
            vmem((TOKENS, 128), F32),
            vmem((8, PLANE, COLS), BF16),
            vmem((HEADS, 8, 16, COLS), BF16),
            vmem((8, 16, COLS), BF16),
            vmem((4, 2, 16, COLS), BF16),
            vmem((BLOCK, WIDTH), BF16),
            pltpu.SemaphoreType.DMA((7,)),
            pltpu.SemaphoreType.DMA((MESSAGES,)),
            pltpu.SemaphoreType.DMA((MESSAGES,)),
            pltpu.SemaphoreType.DMA((4, 2)),
            pltpu.SemaphoreType.DMA((2,)),
        ],
        compiler_params=pltpu.CompilerParams(
            collective_id=0, has_side_effects=True, vmem_limit_bytes=60 * 2 ** 20
        ),
        cost_estimate=pl.CostEstimate(flops=9 * 10 ** 9, bytes_accessed=9 * 2 ** 20, transcendentals=0),
    )(
        head_outputs,
        dec_bias.reshape(1, WIDTH),
        enc_bias.reshape(1, LATS),
        enc_weight,
        dec_weight,
        out_weight,
        active_ids,
    )
    return results[0], results[1]


def solution(mesh):
    return jax.shard_map(
        on_device,
        mesh=mesh,
        in_specs=(
            P("tok", "head"),
            P("head"),
            P("tok"),
            P("head", "tok"),
            P("tok", "head"),
            P("head", "tok"),
            P(),
        ),
        out_specs=(P("tok", "head"), P("tok", "head")),
        check_vma=False,
    )
```

```python
import jax
import jax.numpy as jnp
from jax import lax
from jax.experimental import pallas as pl
from jax.experimental.pallas import tpu as pltpu
from jax.sharding import PartitionSpec as P

MESH = pl.DeviceIdType.MESH
F32, BF16 = jnp.float32, jnp.bfloat16

HEADS = 8
TOKENS, WIDTH, BLOCK = 1024, 1024, 32
LATS, HERE, STRIDE = 2048, 4, 512
COLS = 256
PLANE = 128
PLANES = (0, -1, 1, -2, 2, -3, 3, 4)
SLOT = {0: 0, -1: 1, 1: 2, -2: 3, 2: 4, -3: 5, 3: 6, -4: 7, 4: 7}
GROUPS = ((0, 1), (1, 2), (3, 2), (5, 2), (7, 1))
MESSAGES = 256


def row_of(slot, core, side):
    return PLANE * slot + 64 * core + BLOCK * side


def kernel(
    ho, dbias, ebias, ew, dw, ow, ids,
    both_out,
    ho_v, db_v, eb_v, ew_v, dw_v, ow_v, ids_v,
    cen, off, vals, packed, lat, own_part, core_out, core_in,
    zp_out, zp_in, zm_out, zm_in, x_out, x_in, rec, biases,
    part, part_in, piece, piece_in, proj_v,
    load_sem, send_sem, recv_sem, last_recv, store_sem,
):
    h = lax.axis_index("head")
    t = lax.axis_index("tok")
    core, z, side = t % 2, (t // 2) % 8, t // 16

    def tok_of(dside, dz, dcore):
        return ((side + dside) % 2) * 16 + ((z + dz) % 8) * 2 + (core + dcore) % 2

    zp, zm = {"tok": tok_of(0, 1, 0)}, {"tok": tok_of(0, 7, 0)}
    zp_other, zm_other = {"tok": tok_of(1, 1, 0)}, {"tok": tok_of(1, 7, 0)}
    xn, cn, far = {"tok": tok_of(1, 0, 0)}, {"tok": tok_of(0, 0, 1)}, {"tok": tok_of(0, 4, 0)}
    heads = [(h + k) % HEADS for k in range(HEADS)]
    out_head = t // 4
    my_part = h // 2
    final_tok = [tok_of(my_part % 2, PLANES[s] % 8, my_part // 2) for s in range(8)]
    to_self = (out_head == h) & (my_part == 0)

    loads = []
    for n, (src, dst) in enumerate(
        ((ho, ho_v), (dbias, db_v), (ids, ids_v), (ebias, eb_v), (ew, ew_v), (dw, dw_v), (ow, ow_v))
    ):
        loads.append(pltpu.make_async_copy(src, dst, load_sem.at[n]))
        loads[-1].start()

    barrier = pltpu.get_barrier_semaphore()
    for target in (zp, zm, zp_other, zm_other, xn, cn, far):
        pl.semaphore_signal(barrier, inc=1, device_id=target, device_id_type=MESH)
    for k in range(1, HEADS):
        pl.semaphore_signal(barrier, inc=1, device_id={"head": heads[k]}, device_id_type=MESH)
    for s in range(8):
        target = {"head": out_head, "tok": final_tok[s]}
        pl.semaphore_signal(barrier, inc=1, device_id=target, device_id_type=MESH)

    loads[0].wait()
    loads[1].wait()
    cen[pl.ds(0, BLOCK), :] = (ho_v[...].astype(F32) - db_v[...]).astype(BF16)

    lane = lax.broadcasted_iota(jnp.int32, (PLANE, 128), 1)
    lane_f = lane.astype(F32)

    def offsets(slot):
        def row(q):
            return pl.multiple_of(
                ((side + q % 2) % 2) * 512 + ((z + PLANES[slot] % 8) % 8) * 64 + ((core + q // 2) % 2) * BLOCK,
                BLOCK,
            )

        rows = pl.ds(PLANE * slot, PLANE)
        here = jnp.concatenate([ids_v[pl.ds(row(q), BLOCK), :] for q in range(4)], axis=0)
        here = (here - t * LATS).astype(F32)
        bias = jnp.zeros((PLANE, 128), F32)
        for j in range(HERE):
            column = jnp.sum(jnp.where(lane == t * HERE + j, here, 0.0), axis=1, keepdims=True) - j * STRIDE
            column = jnp.broadcast_to(column, (PLANE, 128))
            off[j, rows, :] = column
            total = jnp.zeros((PLANE, 128), F32)
            for q in range(4):
                first = STRIDE * j + 128 * q
                total += jnp.where(lane_f + 128.0 * q == column, eb_v[:, first:first + 128], 0.0)
            bias += jnp.where(lane == j, jnp.sum(total, axis=1, keepdims=True), 0.0)
        biases[rows, :] = bias

    loads[2].wait()
    loads[3].wait()
    for slot in range(8):
        offsets(slot)
    pl.semaphore_wait(barrier, 7 + 7 + 8)

    sent = []

    def send(src, dst, target):
        n = len(sent)
        copy = pltpu.make_async_remote_copy(
            src_ref=src, dst_ref=dst, send_sem=send_sem.at[n], recv_sem=recv_sem.at[n],
            device_id=target, device_id_type=MESH,
        )
        copy.start()
        sent.append(copy)
        return copy

    def gather(buf, crossed):
        def block(slot, core, side):
            return buf.at[pl.ds(row_of(slot, core, side), BLOCK), :]

        def cross(slot, side):
            crossed[slot, side] = send(block(slot, 0, side), block(slot, 1, side), cn)

        moved = {}

        def go(way, k, side, half):
            if k == 0:
                src = part(0, 0, half)
                target = ((zp, zp_other), (zm, zm_other))[way > 0][side]
            else:
                src = part(SLOT[way * k], side, half)
                target = (zp, zm)[way > 0]
            moved[way, k, side, half] = send(src, part(SLOT[way * (k + 1)], side, half), target)

        def part(slot, side, half):
            return buf.at[pl.ds(row_of(slot, 0, side) + 16 * half, 16), :]

        for side in range(2):
            for half in range(2):
                for way in (-1, 1):
                    go(way, 0, side, half)
        direct = send(block(0, 0, 0), block(7, 0, 0), far)
        over = send(block(0, 0, 0), block(0, 0, 1), xn)
        cross(0, 0)
        yield
        for k in range(1, 4):
            for side in range(2):
                for half in range(2):
                    for way in (-1, 1):
                        moved[way, k - 1, side, half].wait_recv()
                        if k < 3:
                            go(way, k, side, half)
                for way in (-1, 1):
                    cross(SLOT[way * k], side)
                if k == 1 and side == 1:
                    over.wait_recv()
                    cross(0, 1)
                    direct.wait_recv()
                    direct = send(block(7, 0, 0), block(7, 0, 1), xn)
                    cross(7, 0)
                if k == 3 and side == 0:
                    direct.wait_recv()
                    cross(7, 1)
                yield

    def whole(crossed, slots):
        for slot in slots:
            for side in range(2):
                crossed[slot, side].wait_recv()

    crossed = {}
    steps = gather(cen, crossed)
    next(steps)

    def encode(group, latents):
        slot, count = group
        rows = pl.ds(PLANE * slot, PLANE * count)
        lanes = lax.broadcasted_iota(jnp.int32, (PLANE * count, 128), 1)
        lanes_f = lanes.astype(F32)
        picked = jnp.zeros((PLANE * count, 128), F32) if latents[0] == 0 else vals[rows, :]
        for j in latents:
            pre = jnp.dot(
                cen[rows, :], ew_v[:, STRIDE * j:STRIDE * (j + 1)], preferred_element_type=F32
            )
            where = off[j, rows, :]
            total = jnp.zeros((PLANE * count, 128), F32)
            for q in range(4):
                total += jnp.where(lanes_f + 128.0 * q == where, pre[:, 128 * q:128 * (q + 1)], 0.0)
            picked += jnp.where(lanes == j, jnp.sum(total, axis=1, keepdims=True), 0.0)
        vals[rows, :] = picked

    def pack(slots):
        for slot in slots:
            rows = pl.ds(PLANE * slot, PLANE)
            packed[0, :, rows] = vals[rows, :].T[:8, :]
        lanes = pl.ds(PLANE * slots[0], PLANE * len(slots))
        for k in range(1, HEADS):
            arrived[slots[0], k] = send(
                packed.at[0, :, lanes], packed.at[k, :, lanes], {"head": heads[k]}
            )

    arrived = {}
    loads[4].wait()
    next(steps)
    next(steps)
    whole(crossed, (0,))
    encode(GROUPS[0], (0, 1, 2, 3))
    for n in (1, 2):
        slot, count = GROUPS[n]
        next(steps)
        whole(crossed, range(slot, slot + count))
        encode(GROUPS[n], (0, 1))
        next(steps)
        encode(GROUPS[n], (2, 3))
        if n == 1:
            pack((0, 1, 2))
    whole(crossed, (5, 6))
    encode(GROUPS[3], (0, 1, 2, 3))
    pack((5, 6))
    whole(crossed, (7,))
    encode(GROUPS[4], (0, 1, 2, 3))
    pack((7,))
    pack((3, 4))

    loads[5].wait()
    crossed_sums = {}

    def decode(group):
        slot, count = group

        def fill(i, carry):
            rows = pl.ds(pl.multiple_of(PLANE * (slot + i), PLANE), PLANE)
            total = packed[0, :, rows]
            for k in range(1, HEADS):
                total += packed[k, :, rows]
            value = jnp.concatenate([total, jnp.zeros((PLANE - 8, PLANE), F32)], axis=0).T
            value = jnp.maximum(value + biases[rows, :], 0.0)
            for j in range(HERE):
                column = jnp.broadcast_to(value[:, j:j + 1], (PLANE, 128))
                where = off[j, rows, :]
                for q in range(4):
                    lat[pl.ds(pl.multiple_of(PLANE * i, PLANE), PLANE),
                        STRIDE * j + 128 * q:STRIDE * j + 128 * (q + 1)] = jnp.where(
                            lane_f + 128.0 * q == where, column, 0.0).astype(BF16)
            return carry

        lax.fori_loop(0, count, fill, 0)

        total = jnp.dot(lat[pl.ds(0, PLANE * count), :], dw_v[...], preferred_element_type=F32)
        for i in range(count):
            own_part[slot + i] = total[PLANE * i:PLANE * i + 64]
            core_out[slot + i] = total[PLANE * i + 64:PLANE * (i + 1)].astype(BF16)
        for i in range(count):
            crossed_sums[slot + i] = send(core_out.at[slot + i], core_in.at[slot + i], cn)

    def summed(slot, side):
        rows = pl.ds(BLOCK * side, BLOCK)
        return own_part[slot, rows, :] + core_in[slot, rows, :].astype(F32)

    plus, minus = {}, {}

    def ring(out, arrived_at, table, target, n, slot, piece):
        rows = pl.ds(16 * piece, 16)
        total = own_part[slot, rows, :] + core_in[slot, rows, :].astype(F32)
        if n > 3:
            table[n - 4].wait_recv()
            total += arrived_at[n - 4].astype(F32)
        out[n] = total.astype(BF16)
        table[n] = send(out.at[n], arrived_at.at[n], target)

    def ring_step(k):
        for i, piece in enumerate((2, 3, 0, 1)):
            diagonal = k == 1 and piece > 1
            n = 4 * (3 - k) + i
            ring(zp_out, zp_in, plus, zp_other if diagonal else zp, n, SLOT[k], piece)
            ring(zm_out, zm_in, minus, zm_other if diagonal else zm, n, SLOT[-k], piece)

    def get(slot):
        for k in range(1, HEADS):
            arrived[slot, k].wait_recv()

    def meet(*slots):
        for slot in slots:
            crossed_sums[slot].wait_recv()

    get(0)
    decode((0, 1))
    get(5)
    decode((5, 2))
    get(7)
    decode((7, 1))
    meet(5, 6)
    ring_step(3)
    meet(7)
    x_out[0] = summed(7, 1).astype(BF16)
    x_far = send(x_out.at[0], x_in.at[0], xn)
    meet(0)
    x_out[2] = summed(0, 1).astype(BF16)
    x_near = send(x_out.at[2], x_in.at[2], xn)
    get(3)
    decode((3, 2))
    x_far.wait_recv()
    x_out[1] = (summed(7, 0) + x_in[0].astype(F32)).astype(BF16)
    x_far = send(x_out.at[1], x_in.at[1], far)
    meet(3, 4)
    ring_step(2)
    decode((1, 2))
    meet(1, 2)
    ring_step(1)
    mine = summed(0, 0) + db_v[...]
    x_near.wait_recv()
    x_far.wait_recv()
    mine += x_in[1].astype(F32) + x_in[2].astype(F32)
    for half in range(2):
        rows = slice(16 * half, 16 * half + 16)
        total = mine[rows]
        for n in (8 + half, 10 + half):
            plus[n].wait_recv()
            minus[n].wait_recv()
            total += zp_in[n].astype(F32) + zm_in[n].astype(F32)
        rec[rows, :] = total.astype(BF16)

    crossed = {}
    before = len(sent)
    steps = gather(rec, crossed)
    next(steps)
    store_rec = pltpu.make_async_copy(rec.at[pl.ds(0, BLOCK), :], both_out.at[0], store_sem.at[0])
    store_rec.start()
    loads[6].wait()
    for copy in sent[:before]:
        copy.wait_send()
    spread = {}

    def project(group):
        slot, count = group
        out = jnp.dot(
            rec[pl.ds(PLANE * slot, PLANE * count), :], ow_v[...], preferred_element_type=F32
        ).astype(BF16)
        for i in range(count):
            part[slot + i] = out[PLANE * i:PLANE * (i + 1)]
        for k in range(1, HEADS):
            rows = pl.ds(pl.multiple_of(heads[k] * 16, 16), 16)
            spread[slot, k] = send(
                part.at[pl.ds(slot, count), rows, :],
                part_in.at[k, pl.ds(slot, count)],
                {"head": heads[k]},
            )

    def finish(group):
        slot, count = group
        for k in range(1, HEADS):
            spread[slot, k].wait_recv()
        rows = pl.ds(pl.multiple_of(h * 16, 16), 16)
        for s in range(slot, slot + count):
            total = part[s, rows, :].astype(F32)
            for k in range(1, HEADS):
                total += part_in[k, s].astype(F32)
            piece[s] = total.astype(BF16)
            n = len(sent)
            sent.append(None)
            copy = pltpu.make_async_remote_copy(
                src_ref=piece.at[s],
                dst_ref=piece_in.at[t % 4, h % 2],
                send_sem=send_sem.at[n],
                recv_sem=last_recv.at[t % 4, h % 2],
                device_id={"head": out_head, "tok": final_tok[s]},
                device_id_type=MESH,
            )
            if s:
                copy.start()
                sent[n] = copy
                continue
            local = pltpu.make_async_copy(piece.at[0], piece_in.at[t % 4, h % 2], last_recv.at[t % 4, h % 2])

            @pl.when(to_self)
            def _():
                local.start()

            @pl.when(jnp.logical_not(to_self))
            def _():
                copy.start()

            own_piece.append(copy)

    own_piece = []
    next(steps)
    next(steps)
    whole(crossed, (0,))
    project(GROUPS[0])
    next(steps)
    whole(crossed, (1, 2))
    project(GROUPS[1])
    next(steps)
    finish(GROUPS[0])
    next(steps)
    whole(crossed, (3, 4))
    project(GROUPS[2])
    next(steps)
    whole(crossed, (7,))
    project(GROUPS[4])
    whole(crossed, (5, 6))
    project(GROUPS[3])
    finish(GROUPS[1])
    finish(GROUPS[2])
    finish(GROUPS[4])
    finish(GROUPS[3])
    for j in range(4):
        for half in range(2):
            pltpu.make_async_copy(piece_in.at[j, half], piece_in.at[j, half], last_recv.at[j, half]).wait()
            proj_v[16 * half:16 * half + 16, COLS * j:COLS * (j + 1)] = piece_in[j, half]
    store_proj = pltpu.make_async_copy(proj_v, both_out.at[1], store_sem.at[1])
    store_proj.start()
    for copy in sent[before:]:
        if copy is not None:
            copy.wait_send()

    @pl.when(jnp.logical_not(to_self))
    def _():
        own_piece[0].wait_send()

    store_rec.wait()
    store_proj.wait()


def on_device(head_outputs, dec_bias, enc_bias, enc_weight, dec_weight, out_weight, active_ids):
    block = jax.ShapeDtypeStruct((BLOCK, WIDTH), BF16)
    vmem = pltpu.VMEM
    results = pl.pallas_call(
        kernel,
        out_shape=jax.ShapeDtypeStruct((2, BLOCK, WIDTH), BF16),
        in_specs=[pl.BlockSpec(memory_space=pl.ANY)] * 7,
        out_specs=pl.BlockSpec(memory_space=pl.ANY),
        scratch_shapes=[
            vmem((BLOCK, WIDTH), BF16),
            vmem((1, WIDTH), F32),
            vmem((1, LATS), F32),
            vmem((WIDTH, LATS), BF16),
            vmem((LATS, WIDTH), BF16),
            vmem((WIDTH, COLS), BF16),
            vmem((TOKENS, 128), jnp.int32),
            vmem((TOKENS, WIDTH), BF16),
            vmem((HERE, TOKENS, 128), F32),
            vmem((TOKENS, 128), F32),
            vmem((HEADS, 8, TOKENS), F32),
            vmem((2 * PLANE, LATS), BF16),
            vmem((8, 64, WIDTH), F32),
            vmem((8, 64, WIDTH), BF16),
            vmem((8, 64, WIDTH), BF16),
            vmem((12, 16, WIDTH), BF16),
            vmem((12, 16, WIDTH), BF16),
            vmem((12, 16, WIDTH), BF16),
            vmem((12, 16, WIDTH), BF16),
            vmem((3, BLOCK, WIDTH), BF16),
            vmem((3, BLOCK, WIDTH), BF16),
            vmem((TOKENS, WIDTH), BF16),
            vmem((TOKENS, 128), F32),
            vmem((8, PLANE, COLS), BF16),
            vmem((HEADS, 8, 16, COLS), BF16),
            vmem((8, 16, COLS), BF16),
            vmem((4, 2, 16, COLS), BF16),
            vmem((BLOCK, WIDTH), BF16),
            pltpu.SemaphoreType.DMA((7,)),
            pltpu.SemaphoreType.DMA((MESSAGES,)),
            pltpu.SemaphoreType.DMA((MESSAGES,)),
            pltpu.SemaphoreType.DMA((4, 2)),
            pltpu.SemaphoreType.DMA((2,)),
        ],
        compiler_params=pltpu.CompilerParams(
            collective_id=0, has_side_effects=True, vmem_limit_bytes=60 * 2 ** 20
        ),
        cost_estimate=pl.CostEstimate(flops=9 * 10 ** 9, bytes_accessed=9 * 2 ** 20, transcendentals=0),
    )(
        head_outputs,
        dec_bias.reshape(1, WIDTH),
        enc_bias.reshape(1, LATS),
        enc_weight,
        dec_weight,
        out_weight,
        active_ids,
    )
    return results[0], results[1]


def solution(mesh):
    return jax.shard_map(
        on_device,
        mesh=mesh,
        in_specs=(
            P("tok", "head"),
            P("head"),
            P("tok"),
            P("head", "tok"),
            P("tok", "head"),
            P("head", "tok"),
            P(),
        ),
        out_specs=(P("tok", "head"), P("tok", "head")),
        check_vma=False,
    )
```
